32 devices in a mesh: rollout: 4 (over y, x), section: 4 (over z), tensor: 2 (over core).
Axes of the slice: x: 2, y: 2, z: 4, core: 2. Of those that a mesh axis runs over, the one named last changes fastest.
Arguments:
- entering: bfloat16 [4, 128, 8192], P('section', 'tensor', 'rollout')
- arriving: bfloat16 [2, 128, 8192], P(None, 'tensor', 'rollout')
- w_query: bfloat16 [4, 8192, 4096], P('section', 'rollout', 'tensor'), may hold values from -0.0625 to 0.0625
- w_keyval: bfloat16 [4, 8192, 2, 1024], P('section', 'rollout', None, 'tensor'), may hold values from -0.0625 to 0.0625
- w_out: bfloat16 [4, 4096, 8192], P('section', 'tensor', 'rollout'), may hold values from -0.75 to 0.75
- query_bias: bfloat16 [4, 4096], P('section', 'tensor')
- keyval_bias: bfloat16 [4, 2, 1024], P('section', None, 'tensor'), may hold values from -3 to 3
- norm_gain: bfloat16 [4, 8192], P('section', 'rollout'), may hold values from 0.5 to 1.5
- resident_kv: bfloat16 [4, 4, 1120, 2, 1024], P('rollout', 'section', None, None, 'tensor')
- resumed_pages: int32 [4], replicated, may hold values from 24 to 32, as said below
- section_active: int32 [4], replicated, may hold values from 0 to 1, as said below
- block_table: int32 [4, 4, 38, 2], replicated, may hold values from 0 to 37, as said below
Outputs:
- section_out: bfloat16 [4, 3, 128, 8192], P('section', None, 'tensor', 'rollout')
- page_pool: bfloat16 [4, 4, 38, 32, 2, 1024], P('rollout', 'section', None, None, None, 'tensor')
The draws below stay inside these ranges and needn't reach their ends.
Inputs may be any that keep to these rules, and one draw needn't show every extreme that they name: `resumed_pages`: some rollout has exactly 32 pages. `section_active`: exactly 3 sections hold a layer. `block_table`: entry [..., 0] names a decode device (rollout index times 4 plus section index) and entry [..., 1] a slot there; every pair of device and slot is named by exactly one page; the 38 pages of each rollout and section name any one decode device at most 3 times, and each of them reaches that bound for some device.
All inputs are finite; a program needn't handle non-finite values.
Results may differ from the reference program's by a relative error of at most 0.029.
Values may be sent and summed in bfloat16 or wider, within the bound.
A program may use at most 128 MiB of HBM per device.

```python
import functools
import math
import jax
import jax.numpy as jnp
from jax import lax

D = 8192
HQ = 32
KVH = 8
HD = 128
BLOCK = 32
BLOCKS = 3
PAGE = 32
LMAXP = 32
SECTIONS = 4
ROLLOUTS = 4
LAYERS = 3
CTX = 1120
MAXP = 38
DESTS = 16
CAP = 3
N_ROLLOUT = 4
N_TENSOR = 2


def rescale(base, key, rise):
    first, second = jax.random.split(key, 2)
    row_scale = jnp.exp(jax.random.uniform(first, base.shape[:-1] + (1,), jnp.float32, math.log(0.3), math.log(3.0)))
    count = base.shape[-1]
    ramp = jnp.exp((jnp.arange(count, dtype=jnp.float32) / (count - 1) - 0.5) * math.log(rise))
    rough = jnp.exp(jax.random.uniform(second, (count,), jnp.float32, math.log(0.6), math.log(1.6)))
    return (base * row_scale * ramp * rough).astype(jnp.bfloat16)


def draw_entering(key, part):
    key = jax.random.fold_in(key, 21)
    first, second = jax.random.split(key)
    shape = (SECTIONS, ROLLOUTS * BLOCK, D)
    return rescale(jax.random.normal(first, shape, jnp.float32), second, 4.0)


def draw_arriving(key, part):
    key = jax.random.fold_in(key, 22)
    first, second = jax.random.split(key)
    shape = (BLOCKS - 1, ROLLOUTS * BLOCK, D)
    return rescale(jax.random.normal(first, shape, jnp.float32), second, 4.0)


def draw_query_bias(key, part):
    key = jax.random.fold_in(key, 23)
    first = jax.random.fold_in(key, 0)
    noise = jax.random.normal(first, (SECTIONS, HQ, HD), jnp.float32)
    bias = 0.5 * noise
    return bias.reshape(SECTIONS, HQ * HD).astype(jnp.bfloat16)


def draw_resident_kv(key, part):
    key = jax.random.fold_in(key, 24)
    first, second = jax.random.split(key, 2)
    shape = (ROLLOUTS, SECTIONS, CTX, KVH, HD)
    keys = jax.random.normal(first, shape, jnp.float32)
    vals = 1.5 * jax.random.normal(second, shape, jnp.float32)
    return jnp.stack([keys, vals], axis=3).reshape(ROLLOUTS, SECTIONS, CTX, 2, KVH * HD).astype(jnp.bfloat16)


def draw_resumed_pages(key, part):
    key = jax.random.fold_in(key, 31)
    first, second = jax.random.split(key)
    lowest = max(1, 3 * LMAXP // 4)
    pages = jax.random.randint(first, (ROLLOUTS,), lowest, LMAXP + 1)
    chosen = jax.random.randint(second, (), 0, ROLLOUTS)
    return jnp.where(jnp.arange(ROLLOUTS) == chosen, LMAXP, pages).astype(jnp.int32)


def draw_section_active(key, part):
    key = jax.random.fold_in(key, 41)
    order = jax.random.permutation(key, SECTIONS)
    return (order < LAYERS).astype(jnp.int32)


def draw_block_table(key, part):
    key = jax.random.fold_in(key, 51)
    first, second, third, fourth, fifth = jax.random.split(key, 5)
    spots = jax.random.permutation(first, CAP * DESTS)[:MAXP]
    order = jax.random.permutation(second, DESTS)
    placed = jax.random.permutation(third, DESTS)
    turn = jax.random.randint(fourth, (DESTS,), 0, MAXP)
    shuffle = jax.random.permutation(fifth, MAXP)
    residue = (order[:, None] + spots[None, :]) % DESTS
    target = placed[residue]
    slot = (shuffle[None, :] + turn[target]) % MAXP
    return jnp.stack([target, slot], axis=-1).reshape(ROLLOUTS, SECTIONS, MAXP, 2).astype(jnp.int32)


def levels(stream_key, extent, cuts, least, largest):
    def one(position, blocks):
        heights = jax.random.uniform(jax.random.fold_in(jax.random.fold_in(stream_key, 6), position), (blocks,), jnp.float32, least / len(cuts), largest / len(cuts))
        return jnp.repeat(jnp.exp(heights), extent[position] // blocks).reshape((-1,) + (1,) * (len(extent) - position - 1))

    gain = one(*cuts[0])
    for cut in cuts[1:]:
        gain = gain * one(*cut)
    return gain


def scatter_about(stream_key, shape, spread, reach, cuts=(), kind=jnp.bfloat16):
    result = spread * jax.random.normal(stream_key, shape, jnp.float32)
    if cuts:
        result = result * levels(stream_key, shape, cuts, -0.22, 0.18)
    return jnp.clip(result, -reach, reach).astype(kind)


def setup_inputs(seed: int = 0) -> dict:
    seeds = jax.random.split(jax.random.key(seed), 13)
    return {
        "entering": draw_entering(jax.random.fold_in(seeds[12], 71), 0),
        "arriving": draw_arriving(jax.random.fold_in(seeds[12], 71), 0),
        "w_query": scatter_about(seeds[2], (SECTIONS, D, HQ * HD), D ** -0.5, 0.0625, ((0, 4), (1, 4), (2, 2))),
        "w_keyval": scatter_about(seeds[3], (SECTIONS, D, 2, KVH * HD), D ** -0.5, 0.0625, ((0, 4), (1, 4), (3, 2))),
        "w_out": scatter_about(seeds[4], (SECTIONS, HQ * HD, D), (HQ * HD // 64) ** -0.5, 0.75, ((0, 4), (1, 2), (2, 4))),
        "query_bias": draw_query_bias(jax.random.fold_in(seeds[12], 71), 0),
        "keyval_bias": scatter_about(seeds[6], (SECTIONS, 2, KVH * HD), 0.5, 3.0, ((0, 4), (2, 2))),
        "norm_gain": jnp.clip(0.5 + 1.0 * jax.random.uniform(seeds[7], (SECTIONS, D), jnp.float32) ** levels(seeds[7], (SECTIONS, D), ((0, 4), (1, 4)), -0.2, 0.2), 0.5, 1.5).astype(jnp.bfloat16),
        "resident_kv": draw_resident_kv(jax.random.fold_in(seeds[12], 71), 0),
        "resumed_pages": draw_resumed_pages(jax.random.fold_in(seeds[12], 71), 0),
        "section_active": draw_section_active(jax.random.fold_in(seeds[12], 71), 0),
        "block_table": draw_block_table(jax.random.fold_in(seeds[12], 71), 0),
    }


def rotary(values, positions):
    half = HD // 2
    freq = jnp.power(jnp.float32(1000000.0), -(jnp.arange(half, dtype=jnp.float32) * (2.0 / HD)))
    angle = positions.astype(jnp.float32)[:, None] * freq[None, :]
    cosine = jnp.cos(angle)[:, None, :]
    sine = jnp.sin(angle)[:, None, :]
    first = values[..., :half]
    second = values[..., half:]
    return jnp.concatenate([first * cosine - second * sine, second * cosine + first * sine], axis=-1)

def rounded(value):
    return lax.optimization_barrier(value.astype(jnp.bfloat16)).astype(jnp.float32)

def attend(query, cache_keys, cache_vals, new_keys, new_vals, length, step):
    row_count, heads, width = query.shape
    kv_heads = cache_keys.shape[1]
    grouped = query.astype(jnp.float32).reshape(row_count, kv_heads, heads // kv_heads, width)
    scale = 1.0 / math.sqrt(width)
    cached = jnp.einsum('tkgd,jkd->kgtj', grouped, cache_keys.astype(jnp.float32)) * scale
    recent = jnp.einsum('tkgd,jkd->kgtj', grouped, new_keys.astype(jnp.float32)) * scale
    cache_seen = jnp.arange(cache_keys.shape[0], dtype=jnp.int32) < length
    recent_seen = jnp.arange(new_keys.shape[0])[None, :] <= step * row_count + jnp.arange(row_count)[:, None]
    cached = jnp.where(cache_seen, cached, -1e+30)
    recent = jnp.where(recent_seen, recent, -1e+30)
    scores = jnp.concatenate([cached, recent], axis=-1)
    peak = lax.optimization_barrier(jnp.max(scores, axis=-1, keepdims=True))
    powers = jnp.exp(scores - peak)
    weights = (powers / lax.optimization_barrier(jnp.sum(powers, axis=-1, keepdims=True))).astype(jnp.bfloat16)
    values = jnp.concatenate([cache_vals, new_vals], axis=0)
    mixed = jnp.einsum('kgtj,jkd->tkgd', weights.astype(jnp.float32), values.astype(jnp.float32))
    return mixed.reshape(row_count, heads * width).astype(jnp.bfloat16)

def assemble(resident, fresh, start):
    anchor = jnp.zeros((), jnp.int32)
    padded = jnp.concatenate([resident, jnp.zeros_like(fresh)], axis=0)
    padded = lax.dynamic_update_slice(padded, fresh, (start.astype(jnp.int32), anchor, anchor))
    kept_rows = jnp.arange(padded.shape[0], dtype=jnp.int32) < start + fresh.shape[0]
    padded = jnp.where(kept_rows[:, None, None], padded, jnp.zeros_like(padded))
    return padded.reshape(padded.shape[0] // PAGE, PAGE, padded.shape[1], padded.shape[2])

def reference(entering, arriving, w_query, w_keyval, w_out, query_bias, keyval_bias, norm_gain, resident_kv, resumed_pages, section_active, block_table):
    query_width = HQ * HD
    kv_width = KVH * HD
    width_block = D // N_ROLLOUT
    head_group = query_width // N_TENSOR
    token_count = ROLLOUTS * BLOCK
    outputs = [[None] * BLOCKS for _ in range(SECTIONS)]
    fresh_keys = [[] for _ in range(SECTIONS)]
    fresh_vals = [[] for _ in range(SECTIONS)]
    starts = [resumed_pages * PAGE + (SECTIONS - 1 - section) * BLOCK for section in range(SECTIONS)]
    for step in range(BLOCKS):
        for section in range(SECTIONS):
            if step == 0:
                current = entering[section]
            elif section == 0:
                current = arriving[step - 1]
            else:
                current = outputs[section - 1][step - 1]
            xf = current.astype(jnp.float32)
            mean_sq = lax.optimization_barrier(jnp.sum(xf * xf, axis=1, keepdims=True)) / D
            normed = (xf * lax.rsqrt(mean_sq + 1e-06) * norm_gain[section].astype(jnp.float32)).astype(jnp.bfloat16)
            weight_cat = jnp.concatenate([w_query[section], w_keyval[section].reshape(D, 2 * kv_width)], axis=1)
            projected = jnp.zeros((token_count, query_width + 2 * kv_width), jnp.float32)
            for part in range(N_ROLLOUT):
                low = part * width_block
                projected = projected + rounded(jnp.dot(normed[:, low:low + width_block], weight_cat[low:low + width_block], preferred_element_type=jnp.float32))
            query = projected[:, :query_width] + query_bias[section].astype(jnp.float32)
            keys = projected[:, query_width:query_width + kv_width] + keyval_bias[section, 0].astype(jnp.float32)
            vals = projected[:, query_width + kv_width:] + keyval_bias[section, 1].astype(jnp.float32)
            positions = starts[section][:, None] + step * BLOCK + jnp.arange(BLOCK, dtype=jnp.int32)[None, :]
            query = jax.vmap(rotary)(query.reshape(ROLLOUTS, BLOCK, HQ, HD), positions).astype(jnp.bfloat16)
            keys = jax.vmap(rotary)(keys.reshape(ROLLOUTS, BLOCK, KVH, HD), positions).astype(jnp.bfloat16)
            vals = vals.reshape(ROLLOUTS, BLOCK, KVH, HD).astype(jnp.bfloat16)
            fresh_keys[section].append(keys)
            fresh_vals[section].append(vals)
            resident = resident_kv[:, section]
            cache_keys = resident[:, :, 0].reshape(ROLLOUTS, CTX, KVH, HD)
            cache_vals = resident[:, :, 1].reshape(ROLLOUTS, CTX, KVH, HD)
            attended = jax.vmap(functools.partial(attend, step=step))(query, cache_keys, cache_vals, jnp.concatenate(fresh_keys[section], axis=1), jnp.concatenate(fresh_vals[section], axis=1), starts[section])
            attended = attended.reshape(token_count, query_width)
            mixed = jnp.zeros((token_count, D), jnp.float32)
            for part in range(N_TENSOR):
                low = part * head_group
                mixed = mixed + rounded(jnp.dot(attended[:, low:low + head_group], w_out[section, low:low + head_group], preferred_element_type=jnp.float32))
            outputs[section][step] = (xf + section_active[section].astype(jnp.float32) * mixed).astype(jnp.bfloat16)
    pooled = []
    for section in range(SECTIONS):
        fresh = jnp.stack([jnp.concatenate(fresh_keys[section], axis=1).reshape(ROLLOUTS, BLOCKS * BLOCK, kv_width), jnp.concatenate(fresh_vals[section], axis=1).reshape(ROLLOUTS, BLOCKS * BLOCK, kv_width)], axis=2)
        pages = jax.vmap(assemble)(resident_kv[:, section], fresh, starts[section])
        counts = (starts[section] + BLOCKS * BLOCK) // PAGE
        is_live = (jnp.arange(MAXP, dtype=jnp.int32)[None, :] < counts[:, None]) & (section_active[section] > 0)
        pooled.append(jnp.where(is_live[:, :, None, None, None], pages, jnp.zeros_like(pages)))
    pages_all = jnp.stack(pooled, axis=1)
    pool = jnp.zeros((DESTS, MAXP, PAGE, 2, kv_width), jnp.bfloat16)
    pool = pool.at[block_table[..., 0].reshape(-1), block_table[..., 1].reshape(-1)].set(pages_all.reshape(-1, PAGE, 2, kv_width))
    section_out = jnp.stack([jnp.stack(outputs[section]) for section in range(SECTIONS)])
    return (section_out, pool.reshape(ROLLOUTS, SECTIONS, MAXP, PAGE, 2, kv_width))
```

```python
import functools
import math

import jax
import jax.numpy as jnp
from jax import lax
from jax.experimental import pallas as pl
from jax.experimental.pallas import tpu as pltpu
from jax.sharding import PartitionSpec as P

HD = 128
BLOCK = 32
BLOCKS = 3
PAGE = 32
CHUNK = 512
EPS = 1e-06
MESH = pl.DeviceIdType.MESH


def remote(src, dst, send, recv, **where):
    return pltpu.make_async_remote_copy(
        src_ref=src, dst_ref=dst, send_sem=send, recv_sem=recv, device_id=where, device_id_type=MESH
    )


def steps_kernel(
    dims,
    info,
    entering,
    arriving,
    gain,
    query_bias,
    keyval_bias,
    cosine,
    sine,
    w_query,
    w_keyval,
    w_out,
    cache_keys,
    cache_vals,
    packed,
    out,
    landed,
    fresh,
    wcat,
    wout,
    keys,
    vals,
    own_x,
    peer_x,
    normed,
    part,
    squares,
    part_in,
    squares_in,
    heads,
    attended,
    mixed,
    mixed_in,
    page_wide,
    page,
    load_sem,
    fwd_s,
    fwd_r,
    sq_s,
    sq_r,
    rs_s,
    rs_r,
    ag_s,
    ag_r,
    ex_s,
    ex_r,
    hand_s,
    hand_r,
    ship_s,
    ship_r,
    fz_s,
    fz_r,
    fx_s,
    fx_r,
    own_sem,
):
    R, S, context = dims
    r = lax.axis_index("rollout")
    s = lax.axis_index("section")
    t = lax.axis_index("tensor")
    other = 1 - t
    token_rows, width = entering.shape
    qw = w_query.shape[1]
    kw = cache_keys.shape[1]
    dests = R * S
    me = r * S + s
    n_rs = wcat.shape[1] // CHUNK
    n_out = wout.shape[1] // CHUNK
    n_kv = kw // HD
    group = qw // kw
    group_width = group * HD
    half = token_rows

    loads = [
        pltpu.make_async_copy(w_query, wcat.at[:, pl.ds(0, qw)], load_sem.at[0]),
        pltpu.make_async_copy(w_keyval, wcat.at[:, pl.ds(qw, 2 * kw)], load_sem.at[1]),
        pltpu.make_async_copy(w_out, wout, load_sem.at[2]),
        pltpu.make_async_copy(cache_keys, keys.at[pl.ds(0, context)], load_sem.at[3]),
        pltpu.make_async_copy(cache_vals, vals.at[pl.ds(0, context)], load_sem.at[4]),
    ]
    for load in loads:
        load.start()

    barrier = pltpu.get_barrier_semaphore()

    def greet(o, carry):
        d = lax.rem(me + o, dests)
        pl.semaphore_signal(
            barrier, inc=1, device_id={"rollout": d // S, "section": lax.rem(d, S)}, device_id_type=MESH
        )
        return carry

    lax.fori_loop(1, dests, greet, 0)
    pl.semaphore_signal(barrier, inc=1, device_id={"tensor": other}, device_id_type=MESH)

    own_x[0] = entering[...]

    @pl.when(s == 0)
    def _():
        for k in range(1, BLOCKS):
            own_x[k] = arriving[k - 1]

    spare = keys.shape[0] - context
    keys[pl.ds(context, spare), :] = jnp.zeros((spare, kw), jnp.bfloat16)
    vals[pl.ds(context, spare), :] = jnp.zeros((spare, kw), jnp.bfloat16)
    pl.semaphore_wait(barrier, dests)

    def cols(c, size=CHUNK):
        return pl.ds(pl.multiple_of(c * size, size), size)

    def rows_of(b):
        return pl.ds(pl.multiple_of(b * BLOCK, BLOCK), BLOCK)

    def fwd(k, c):
        return remote(own_x.at[k, :, cols(c)], peer_x.at[:, cols(c)], fwd_s.at[c], fwd_r.at[c], tensor=other)

    def hand(k, c):
        return remote(
            out.at[k, :, cols(c)],
            own_x.at[k + 1, :, cols(c)],
            hand_s.at[k, c],
            hand_r.at[k, c],
            section=jnp.minimum(s + 1, S - 1),
        )

    def ahead(j):
        return lax.rem(r + j, R)

    def behind(j):
        return lax.rem(r + R - j, R)

    def sq(j):
        return remote(
            squares.at[rows_of(ahead(j))], squares_in.at[rows_of(r)], sq_s.at[j], sq_r.at[j], rollout=ahead(j)
        )

    def rs(c, j):
        return remote(
            part.at[rows_of(ahead(j)), cols(c)],
            part_in.at[rows_of(r), cols(c)],
            rs_s.at[c, j],
            rs_r.at[c, j],
            rollout=ahead(j),
        )

    def ag(c, j):
        ref = attended.at[rows_of(r), cols(c, group_width)]
        return remote(ref, ref, ag_s.at[c, j], ag_r.at[c, j], rollout=ahead(j))

    def ex(c):
        return remote(
            mixed.at[pl.ds(pl.multiple_of(other * half, BLOCK), half), cols(c)],
            mixed_in.at[:, cols(c)],
            ex_s.at[c],
            ex_r.at[c],
            tensor=other,
        )

    def ship(o):
        d = lax.rem(me + o, dests)
        return remote(
            packed.at[d], landed.at[me], ship_s.at[o], ship_r.at[o], rollout=d // S, section=lax.rem(d, S)
        )

    def fz(k, j):
        return remote(
            page.at[k], fresh.at[k, r, s], fz_s.at[k, j], fz_r.at[k, j], section=lax.rem(s + j, S)
        )

    def fx(k, j):
        return remote(fresh.at[k, r], fresh.at[k, r], fx_s.at[k, j], fx_r.at[k, j], rollout=ahead(j))

    def own_page(k):
        return pltpu.make_async_copy(page.at[k], fresh.at[k, r, s], own_sem.at[k])

    own_slots = pltpu.make_async_copy(packed.at[me], landed.at[me], own_sem.at[BLOCKS])
    own_slots.start()

    def spread(k):
        own_page(k).wait()
        for j in range(1, S):
            fz(k, j).wait()
        for j in range(1, R):
            fx(k, j).start()

    share = (dests - 1 + BLOCKS - 1) // BLOCKS

    def step_body(k, carry):
        for c in range(n_out):
            @pl.when((k > 0) & (s > 0))
            def _(c=c):
                hand(k - 1, c).wait_recv()

            fwd(k, c).start()

        def norm(ref, base):
            def body(i, carry):
                xf = ref[rows_of(i), :].astype(jnp.float32)
                ms = jnp.sum(xf * xf, axis=1, keepdims=True) / width
                rows = pl.ds(pl.multiple_of(base + i * BLOCK, BLOCK), BLOCK)
                normed[rows, :] = (xf * lax.rsqrt(ms + EPS) * gain[...].astype(jnp.float32)).astype(
                    jnp.bfloat16
                )
                squares[rows, :] = jnp.broadcast_to(ms, (BLOCK, HD))
                return carry

            lax.fori_loop(0, half // BLOCK, body, 0)

        norm(own_x.at[k], t * half)
        for c in range(n_out):
            fwd(k, c).wait()
        norm(peer_x, other * half)
        for j in range(1, R):
            sq(j).start()

        @pl.when(k == 0)
        def _():
            loads[0].wait()
            loads[1].wait()

        def project(c, carry):
            part[:, cols(c)] = jnp.dot(
                normed[...], wcat[:, cols(c)], preferred_element_type=jnp.float32
            ).astype(jnp.bfloat16)
            for j in range(1, R):
                rs(c, j).start()
            return carry

        lax.fori_loop(0, n_rs, project, 0)

        def ship_some(o, carry):
            ship(o).start()
            return carry

        lax.fori_loop(1 + k * share, jnp.minimum(1 + (k + 1) * share, dests), ship_some, 0)

        @pl.when(k > 0)
        def _():
            spread(k - 1)

        for j in range(1, R):
            sq(j).wait()
        ms = [squares[rows_of(r), :]] + [squares_in[rows_of(behind(j)), :] for j in range(1, R)]
        whole = lax.rsqrt(sum(ms) / R + EPS)
        ratios = []
        for m in ms:
            local = lax.rsqrt(m + EPS)
            ratios.append(jnp.where(local > 0, whole / jnp.where(local > 0, local, 1.0), 0.0)[:, :1])
        cos = cosine[pl.ds(pl.multiple_of(k * BLOCK, BLOCK), BLOCK), :]
        sin = sine[pl.ds(pl.multiple_of(k * BLOCK, BLOCK), BLOCK), :]

        def rotate(v):
            return v * cos + pltpu.roll(v, HD // 2, 1) * sin

        new_rows = pl.ds(pl.multiple_of(context + k * BLOCK, BLOCK), BLOCK)
        for c in range(n_rs):
            for j in range(1, R):
                rs(c, j).wait()
            acc = part[rows_of(r), cols(c)].astype(jnp.float32) * ratios[0]
            for j in range(1, R):
                acc = acc + part_in[rows_of(behind(j)), cols(c)].astype(jnp.float32) * ratios[j]
            low = c * CHUNK
            for h in range(CHUNK // HD):
                at = low + h * HD
                one = acc[:, h * HD : (h + 1) * HD]
                if at < qw:
                    one = rotate(one + query_bias[:, at : at + HD].astype(jnp.float32))
                    heads[at // HD * BLOCK : (at // HD + 1) * BLOCK, :] = one.astype(jnp.bfloat16)
                else:
                    at = at - qw
                    one = one + keyval_bias[:, at : at + HD].astype(jnp.float32)
                    if at < kw:
                        one = rotate(one)
                    kind, at = at // kw, at % kw
                    target = keys if kind == 0 else vals
                    target[new_rows, at : at + HD] = one.astype(jnp.bfloat16)
                    page_wide[:, kind, at : at + HD] = one
        page[k] = page_wide[...].astype(jnp.bfloat16)
        own_page(k).start()
        for j in range(1, S):
            fz(k, j).start()

        @pl.when(k == 0)
        def _():
            loads[3].wait()
            loads[4].wait()

        total = keys.shape[0]
        column = lax.broadcasted_iota(jnp.int32, (group * BLOCK, total), 1)
        token = lax.rem(lax.broadcasted_iota(jnp.int32, (group * BLOCK, total), 0), BLOCK)
        seen = (column < info[0]) | ((column >= context) & (column - context <= k * BLOCK + token))
        for g in range(n_kv):
            at = g * HD
            scores = lax.dot_general(
                heads[g * group * BLOCK : (g + 1) * group * BLOCK, :],
                keys[:, at : at + HD],
                (((1,), (1,)), ((), ())),
                preferred_element_type=jnp.float32,
            )
            scores = jnp.where(seen, scores * (1.0 / math.sqrt(HD)), -1e30)
            powers = jnp.exp(scores - jnp.max(scores, axis=-1, keepdims=True))
            total_power = jnp.sum(powers, axis=-1, keepdims=True)
            got = jnp.dot(
                powers.astype(jnp.bfloat16), vals[:, at : at + HD], preferred_element_type=jnp.float32
            )
            got = (got / total_power).astype(jnp.bfloat16)
            for i in range(group):
                lane = (g * group + i) * HD
                attended[rows_of(r), lane : lane + HD] = got[i * BLOCK : (i + 1) * BLOCK, :]
            for j in range(1, R):
                ag(g, j).start()

        @pl.when(k == 0)
        def _():
            loads[2].wait()

        for g in range(n_kv):
            for j in range(1, R):
                ag(g, j).wait()

        def project_out(c, carry):
            mixed[:, cols(c)] = jnp.dot(
                attended[...], wout[:, cols(c)], preferred_element_type=jnp.float32
            ).astype(jnp.bfloat16)
            ex(c).start()
            return carry

        lax.fori_loop(0, n_out, project_out, 0)
        active = info[1].astype(jnp.float32)

        def finish(c, carry):
            ex(c).wait()
            own = mixed[pl.ds(pl.multiple_of(t * half, BLOCK), half), cols(c)].astype(jnp.float32)
            summed = own + mixed_in[:, cols(c)].astype(jnp.float32)
            base = own_x[k, :, cols(c)].astype(jnp.float32)
            out[k, :, cols(c)] = (base + active * summed).astype(jnp.bfloat16)

            @pl.when((k < BLOCKS - 1) & (s < S - 1))
            def _():
                hand(k, c).start()

            return carry

        lax.fori_loop(0, n_out, finish, 0)
        return carry

    lax.fori_loop(0, BLOCKS, step_body, 0)
    spread(BLOCKS - 1)

    @pl.when(s < S - 1)
    def _():
        for k in range(BLOCKS - 1):
            for c in range(n_out):
                hand(k, c).wait_send()

    def ship_wait(o, carry):
        ship(o).wait()
        return carry

    lax.fori_loop(1, dests, ship_wait, 0)
    own_slots.wait()
    for k in range(BLOCKS):
        for j in range(1, R):
            fx(k, j).wait()


def pack_kernel(slots, pages, source, packed, sem):
    def copy(i):
        return pltpu.make_async_copy(source.at[pages[i]], packed.at[i], sem.at[i])

    def start(i, carry):
        copy(i).start()
        return carry

    def finish(i, carry):
        copy(i).wait()
        return carry

    lax.fori_loop(0, slots, start, 0)
    lax.fori_loop(0, slots, finish, 0)


def place_kernel(slots, kind, place, landed, fresh, pool, zero, sem):
    zero[...] = jnp.zeros_like(zero)

    def start(i, carry):
        @pl.when(kind[i] == 0)
        def _():
            pltpu.make_async_copy(zero, pool.at[i], sem.at[i]).start()

        @pl.when(kind[i] == 1)
        def _():
            pltpu.make_async_copy(landed.at[place[i]], pool.at[i], sem.at[i]).start()

        @pl.when(kind[i] == 2)
        def _():
            pltpu.make_async_copy(fresh.at[place[i]], pool.at[i], sem.at[i]).start()

        return carry

    def finish(i, carry):
        pltpu.make_async_copy(zero, pool.at[i], sem.at[i]).wait()
        return carry

    lax.fori_loop(0, slots, start, 0)
    lax.fori_loop(0, slots, finish, 0)


def local(
    entering,
    arriving,
    w_query,
    w_keyval,
    w_out,
    query_bias,
    keyval_bias,
    norm_gain,
    resident_kv,
    resumed_pages,
    section_active,
    block_table,
):
    R = lax.axis_size("rollout")
    S = lax.axis_size("section")
    r = lax.axis_index("rollout")
    s = lax.axis_index("section")
    width_block, qw = w_query.shape[1:]
    kw = w_keyval.shape[3]
    token_rows = entering.shape[1]
    rows = R * BLOCK
    out_width = w_out.shape[2]
    context = resident_kv.shape[2]
    page_count = block_table.shape[2]
    dests = R * S
    cap = (page_count + dests - 1) // dests
    me = r * S + s
    first_page = resumed_pages[r] + (S - 1 - s)
    length = first_page * PAGE

    routing = block_table.reshape(dests, page_count, 2)
    targets = routing[:, :, 0]
    slot_ids = routing[:, :, 1]
    page_ids = jnp.arange(page_count, dtype=jnp.int32)
    before = page_ids[None, :] < page_ids[:, None]
    ranks = jnp.sum(
        ((targets[:, :, None] == targets[:, None, :]) & before[None]).astype(jnp.int32), axis=2
    )
    column = targets[me] * cap + ranks[me]
    buffer_ids = jnp.arange(dests * cap, dtype=jnp.int32)
    source_pages = jnp.minimum(page_ids, context // PAGE - 1)
    pack_pages = jnp.sum(
        jnp.where(buffer_ids[:, None] == column[None, :], source_pages[None, :], 0), axis=1
    ).astype(jnp.int32)
    sources = jnp.arange(dests, dtype=jnp.int32)
    first_of = resumed_pages[sources // S] + (S - 1 - sources % S)
    turn = page_ids[None, :] - first_of[:, None]
    alive = (turn < BLOCKS) & (section_active[sources % S] > 0)[:, None]
    kinds = jnp.where(alive, jnp.where(turn >= 0, 2, 1), 0)
    places = jnp.where(
        kinds == 2,
        jnp.clip(turn, 0, BLOCKS - 1) * dests + sources[:, None],
        sources[:, None] * cap + jnp.minimum(ranks, cap - 1),
    )
    codes = (kinds * (BLOCKS * dests + dests * cap) + places).reshape(-1)
    hit = (targets == me).reshape(-1)[None, :] & (slot_ids.reshape(-1)[None, :] == page_ids[:, None])
    code = jnp.sum(jnp.where(hit, codes[None, :], 0), axis=1).astype(jnp.int32)
    base = BLOCKS * dests + dests * cap
    kind, place = code // base, code % base

    positions = (length + jnp.arange(BLOCKS * BLOCK, dtype=jnp.int32)).astype(jnp.float32)
    freq = jnp.power(
        jnp.float32(1000000.0), -(jnp.arange(HD // 2, dtype=jnp.float32) * (2.0 / HD))
    )
    angle = positions[:, None] * freq[None, :]
    cosine = jnp.cos(angle)
    sine = jnp.sin(angle)
    cosine = jnp.concatenate([cosine, cosine], axis=1)
    sine = jnp.concatenate([-sine, sine], axis=1)
    info = jnp.stack([length, section_active[s]]).astype(jnp.int32)

    resident = resident_kv[0, 0]
    page_shape = (PAGE, 2, kw)
    bf16 = jnp.bfloat16
    f32 = jnp.float32
    anywhere = pl.BlockSpec(memory_space=pl.ANY)
    vmem = pl.BlockSpec(memory_space=pltpu.VMEM)
    smem = pl.BlockSpec(memory_space=pltpu.SMEM)
    dma = pltpu.SemaphoreType.DMA

    packed = pl.pallas_call(
        functools.partial(pack_kernel, dests * cap),
        out_shape=jax.ShapeDtypeStruct((dests * cap,) + page_shape, bf16),
        in_specs=[smem, anywhere],
        out_specs=anywhere,
        scratch_shapes=[dma((dests * cap,))],
        name="pack_pages",
    )(pack_pages, resident.reshape((context // PAGE,) + page_shape))

    total = -(-(context + BLOCKS * BLOCK) // HD) * HD
    n_rs = (qw + 2 * kw) // CHUNK
    n_out = out_width // CHUNK
    n_kv = kw // HD
    section_out, landed, fresh = pl.pallas_call(
        functools.partial(steps_kernel, (R, S, context)),
        out_shape=(
            jax.ShapeDtypeStruct((BLOCKS, token_rows, out_width), bf16),
            jax.ShapeDtypeStruct((dests, cap) + page_shape, bf16),
            jax.ShapeDtypeStruct((BLOCKS, R, S) + page_shape, bf16),
        ),
        in_specs=[smem] + [vmem] * 7 + [anywhere] * 6,
        out_specs=(vmem, anywhere, anywhere),
        scratch_shapes=[
            pltpu.VMEM((width_block, qw + 2 * kw), bf16),
            pltpu.VMEM((qw, out_width), bf16),
            pltpu.VMEM((total, kw), bf16),
            pltpu.VMEM((total, kw), bf16),
            pltpu.VMEM((BLOCKS, token_rows, width_block), bf16),
            pltpu.VMEM((token_rows, width_block), bf16),
            pltpu.VMEM((rows, width_block), bf16),
            pltpu.VMEM((rows, qw + 2 * kw), bf16),
            pltpu.VMEM((rows, HD), f32),
            pltpu.VMEM((rows, qw + 2 * kw), bf16),
            pltpu.VMEM((rows, HD), f32),
            pltpu.VMEM((qw // HD * BLOCK, HD), bf16),
            pltpu.VMEM((rows, qw), bf16),
            pltpu.VMEM((rows, out_width), bf16),
            pltpu.VMEM((token_rows, out_width), bf16),
            pltpu.VMEM(page_shape, f32),
            pltpu.VMEM((BLOCKS,) + page_shape, bf16),
            dma((5,)),
            dma((n_out,)),
            dma((n_out,)),
            dma((R,)),
            dma((R,)),
            dma((n_rs, R)),
            dma((n_rs, R)),
            dma((n_kv, R)),
            dma((n_kv, R)),
            dma((n_out,)),
            dma((n_out,)),
            dma((BLOCKS, n_out)),
            dma((BLOCKS, n_out)),
            dma((dests,)),
            dma((dests,)),
            dma((BLOCKS, S)),
            dma((BLOCKS, S)),
            dma((BLOCKS, R)),
            dma((BLOCKS, R)),
            dma((BLOCKS + 1,)),
        ],
        compiler_params=pltpu.CompilerParams(
            collective_id=0, has_side_effects=True, vmem_limit_bytes=60 * 1024 * 1024
        ),
        name="relay_steps",
    )(
        info,
        entering[0],
        arriving,
        norm_gain,
        query_bias,
        keyval_bias.reshape(1, 2 * kw),
        cosine,
        sine,
        w_query[0],
        w_keyval[0].reshape(width_block, 2 * kw),
        w_out[0],
        resident[:, 0],
        resident[:, 1],
        packed.reshape((dests, cap) + page_shape),
    )

    pool = pl.pallas_call(
        functools.partial(place_kernel, page_count),
        out_shape=jax.ShapeDtypeStruct((page_count,) + page_shape, bf16),
        in_specs=[smem, smem, anywhere, anywhere],
        out_specs=anywhere,
        scratch_shapes=[pltpu.VMEM(page_shape, bf16), dma((page_count,))],
        name="place_pages",
    )(
        kind,
        place,
        landed.reshape((dests * cap,) + page_shape),
        fresh.reshape((BLOCKS * dests,) + page_shape),
    )
    return (section_out[None], pool[None, None])


def solution(mesh):
    in_specs = (
        P("section", "tensor", "rollout"),
        P(None, "tensor", "rollout"),
        P("section", "rollout", "tensor"),
        P("section", "rollout", None, "tensor"),
        P("section", "tensor", "rollout"),
        P("section", "tensor"),
        P("section", None, "tensor"),
        P("section", "rollout"),
        P("rollout", "section", None, None, "tensor"),
        P(),
        P(),
        P(),
    )
    out_specs = (
        P("section", None, "tensor", "rollout"),
        P("rollout", "section", None, None, None, "tensor"),
    )
    return jax.shard_map(local, mesh=mesh, in_specs=in_specs, out_specs=out_specs, check_vma=False)
```

```python
import functools
import math

import jax
import jax.numpy as jnp
from jax import lax
from jax.experimental import pallas as pl
from jax.experimental.pallas import tpu as pltpu
from jax.sharding import PartitionSpec as P

HD = 128
BLOCK = 32
BLOCKS = 3
PAGE = 32
CHUNK = 512
EPS = 1e-06
MESH = pl.DeviceIdType.MESH


def remote(src, dst, send, recv, **where):
    return pltpu.make_async_remote_copy(
        src_ref=src, dst_ref=dst, send_sem=send, recv_sem=recv, device_id=where, device_id_type=MESH
    )


def steps_kernel(
    dims,
    resumed,
    layer_on,
    pack_pages,
    entering,
    arriving,
    gain,
    query_bias,
    keyval_bias,
    freq,
    w_query,
    w_keyval,
    w_out,
    resident,
    out,
    landed,
    fresh,
    wcat,
    wout,
    kv,
    packed,
    own_x,
    peer_x,
    normed,
    part,
    squares,
    part_in,
    squares_in,
    heads,
    attended,
    mixed,
    mixed_in,
    load_sem,
    fwd_s,
    fwd_r,
    sq_s,
    sq_r,
    rs_s,
    rs_r,
    ag_s,
    ag_r,
    ex_s,
    ex_r,
    hand_s,
    hand_r,
    ship_s,
    ship_r,
    fz_s,
    fz_r,
    fx_s,
    fx_r,
    own_sem,
):
    R, S, context = dims
    r = lax.axis_index("rollout")
    s = lax.axis_index("section")
    t = lax.axis_index("tensor")
    other = 1 - t
    token_rows, width = entering.shape
    qw = w_query.shape[1]
    kw = resident.shape[2] // 2
    held = resident.shape[0]
    dests = R * S
    me = r * S + s
    n_rs = wcat.shape[1] // CHUNK
    n_out = wout.shape[1] // CHUNK
    n_kv = kw // HD
    group = qw // kw
    group_width = group * HD
    half = token_rows
    length = (resumed[r] + (S - 1 - s)) * PAGE

    loads = [
        pltpu.make_async_copy(w_query, wcat.at[:, pl.ds(0, qw)], load_sem.at[0]),
        pltpu.make_async_copy(w_keyval, wcat.at[:, pl.ds(qw, 2 * kw)], load_sem.at[1]),
        pltpu.make_async_copy(w_out, wout, load_sem.at[2]),
        pltpu.make_async_copy(resident, kv.at[pl.ds(0, held)], load_sem.at[3]),
    ]
    for load in loads:
        load.start()

    barrier = pltpu.get_barrier_semaphore()

    def greet(o, carry):
        d = lax.rem(me + o, dests)
        pl.semaphore_signal(
            barrier, inc=1, device_id={"rollout": d // S, "section": lax.rem(d, S)}, device_id_type=MESH
        )
        return carry

    lax.fori_loop(1, dests, greet, 0)
    pl.semaphore_signal(barrier, inc=1, device_id={"tensor": other}, device_id_type=MESH)

    own_x[0] = entering[...]

    @pl.when(s == 0)
    def _():
        for k in range(1, BLOCKS):
            own_x[k] = arriving[k - 1]

    spare = kv.shape[0] - held
    kv[pl.ds(held, spare)] = jnp.zeros((spare, PAGE, 2 * kw), jnp.bfloat16)
    pl.semaphore_wait(barrier, dests)

    def cols(c, size=CHUNK):
        return pl.ds(pl.multiple_of(c * size, size), size)

    def rows_of(b):
        return pl.ds(pl.multiple_of(b * BLOCK, BLOCK), BLOCK)

    def fwd(k, c):
        return remote(own_x.at[k, :, cols(c)], peer_x.at[:, cols(c)], fwd_s.at[c], fwd_r.at[c], tensor=other)

    def hand(k, c):
        return remote(
            out.at[k, :, cols(c)],
            own_x.at[k + 1, :, cols(c)],
            hand_s.at[k, c],
            hand_r.at[k, c],
            section=jnp.minimum(s + 1, S - 1),
        )

    def ahead(j):
        return lax.rem(r + j, R)

    def behind(j):
        return lax.rem(r + R - j, R)

    def sq(j):
        return remote(
            squares.at[rows_of(ahead(j))], squares_in.at[rows_of(r)], sq_s.at[j], sq_r.at[j], rollout=ahead(j)
        )

    def rs(c, j):
        return remote(
            part.at[rows_of(ahead(j)), cols(c)],
            part_in.at[rows_of(r), cols(c)],
            rs_s.at[c, j],
            rs_r.at[c, j],
            rollout=ahead(j),
        )

    def ag(c, j):
        ref = attended.at[rows_of(r), cols(c, group_width)]
        return remote(ref, ref, ag_s.at[c, j], ag_r.at[c, j], rollout=ahead(j))

    def ex(c):
        return remote(
            mixed.at[pl.ds(pl.multiple_of(other * half, BLOCK), half), cols(c)],
            mixed_in.at[:, cols(c)],
            ex_s.at[c],
            ex_r.at[c],
            tensor=other,
        )

    def ship(o):
        d = lax.rem(me + o, dests)
        return remote(
            packed.at[d], landed.at[me], ship_s.at[o], ship_r.at[o], rollout=d // S, section=lax.rem(d, S)
        )

    def fz(k, j):
        return remote(
            kv.at[held + k], fresh.at[k, r, s], fz_s.at[k, j], fz_r.at[k, j], section=lax.rem(s + j, S)
        )

    def fx(k, j):
        return remote(fresh.at[k, r], fresh.at[k, r], fx_s.at[k, j], fx_r.at[k, j], rollout=ahead(j))

    def own_page(k):
        return pltpu.make_async_copy(kv.at[held + k], fresh.at[k, r, s], own_sem.at[k])

    own_slots = pltpu.make_async_copy(packed.at[me], landed.at[me], own_sem.at[BLOCKS])

    def spread(k):
        own_page(k).wait()
        for j in range(1, S):
            fz(k, j).wait()
        for j in range(1, R):
            fx(k, j).start()

    share = (dests - 1 + BLOCKS - 1) // BLOCKS

    def step_body(k, carry):
        for c in range(n_out):
            @pl.when((k > 0) & (s > 0))
            def _(c=c):
                hand(k - 1, c).wait_recv()

            fwd(k, c).start()

        def norm(ref, base):
            def body(i, carry):
                xf = ref[rows_of(i), :].astype(jnp.float32)
                ms = jnp.sum(xf * xf, axis=1, keepdims=True) / width
                rows = pl.ds(pl.multiple_of(base + i * BLOCK, BLOCK), BLOCK)
                normed[rows, :] = (xf * lax.rsqrt(ms + EPS) * gain[...].astype(jnp.float32)).astype(
                    jnp.bfloat16
                )
                squares[rows, :] = jnp.broadcast_to(ms, (BLOCK, HD))
                return carry

            lax.fori_loop(0, half // BLOCK, body, 0)

        norm(own_x.at[k], t * half)
        for c in range(n_out):
            fwd(k, c).wait()
        norm(peer_x, other * half)
        for j in range(1, R):
            sq(j).start()

        @pl.when(k == 0)
        def _():
            loads[0].wait()
            loads[1].wait()

        def project(c, carry):
            part[:, cols(c)] = jnp.dot(
                normed[...], wcat[:, cols(c)], preferred_element_type=jnp.float32
            ).astype(jnp.bfloat16)
            for j in range(1, R):
                rs(c, j).start()
            return carry

        lax.fori_loop(0, n_rs, project, 0)

        @pl.when(k == 0)
        def _():
            loads[3].wait()

            def pack(d, carry):
                for c in range(packed.shape[1]):
                    packed[d, c] = kv[pack_pages[d * packed.shape[1] + c]]
                return carry

            lax.fori_loop(0, dests, pack, 0)
            own_slots.start()

        def ship_some(o, carry):
            ship(o).start()
            return carry

        lax.fori_loop(1 + k * share, jnp.minimum(1 + (k + 1) * share, dests), ship_some, 0)

        @pl.when(k > 0)
        def _():
            spread(k - 1)

        for j in range(1, R):
            sq(j).wait()
        ms = [squares[rows_of(r), :]] + [squares_in[rows_of(behind(j)), :] for j in range(1, R)]
        whole = lax.rsqrt(sum(ms) / R + EPS)
        ratios = []
        for m in ms:
            local = lax.rsqrt(m + EPS)
            ratios.append(jnp.where(local > 0, whole / jnp.where(local > 0, local, 1.0), 0.0)[:, :1])
        angle = (length + k * BLOCK + lax.broadcasted_iota(jnp.int32, (BLOCK, HD), 0)).astype(
            jnp.float32
        ) * freq[...]
        lane = lax.broadcasted_iota(jnp.int32, (BLOCK, HD), 1)
        cos = jnp.cos(angle)
        sin = jnp.sin(angle)
        sin = jnp.where(lane < HD // 2, -sin, sin)

        def rotate(v):
            return v * cos + pltpu.roll(v, HD // 2, 1) * sin

        for c in range(n_rs):
            for j in range(1, R):
                rs(c, j).wait()
            acc = part[rows_of(r), cols(c)].astype(jnp.float32) * ratios[0]
            for j in range(1, R):
                acc = acc + part_in[rows_of(behind(j)), cols(c)].astype(jnp.float32) * ratios[j]
            low = c * CHUNK
            for h in range(CHUNK // HD):
                at = low + h * HD
                one = acc[:, h * HD : (h + 1) * HD]
                if at < qw:
                    one = rotate(one + query_bias[:, at : at + HD].astype(jnp.float32))
                    heads[at // HD * BLOCK : (at // HD + 1) * BLOCK, :] = one.astype(jnp.bfloat16)
                else:
                    at = at - qw
                    one = one + keyval_bias[:, at : at + HD].astype(jnp.float32)
                    if at < kw:
                        one = rotate(one)
                    kv[held + k, :, at : at + HD] = one.astype(jnp.bfloat16)
        own_page(k).start()
        for j in range(1, S):
            fz(k, j).start()

        total = kv.shape[0] * PAGE
        column = lax.broadcasted_iota(jnp.int32, (group * BLOCK, total), 1)
        token = lax.rem(lax.broadcasted_iota(jnp.int32, (group * BLOCK, total), 0), BLOCK)
        seen = (column < length) | ((column >= context) & (column - context <= k * BLOCK + token))
        for g in range(n_kv):
            at = g * HD
            scores = lax.dot_general(
                heads[g * group * BLOCK : (g + 1) * group * BLOCK, :],
                kv[:, :, at : at + HD].reshape(total, HD),
                (((1,), (1,)), ((), ())),
                preferred_element_type=jnp.float32,
            )
            scores = jnp.where(seen, scores * (1.0 / math.sqrt(HD)), -1e30)
            powers = jnp.exp(scores - jnp.max(scores, axis=-1, keepdims=True))
            total_power = jnp.sum(powers, axis=-1, keepdims=True)
            got = jnp.dot(
                powers.astype(jnp.bfloat16),
                kv[:, :, kw + at : kw + at + HD].reshape(total, HD),
                preferred_element_type=jnp.float32,
            )
            got = (got / total_power).astype(jnp.bfloat16)
            for i in range(group):
                lane = (g * group + i) * HD
                attended[rows_of(r), lane : lane + HD] = got[i * BLOCK : (i + 1) * BLOCK, :]
            for j in range(1, R):
                ag(g, j).start()

        @pl.when(k == 0)
        def _():
            loads[2].wait()

        for g in range(n_kv):
            for j in range(1, R):
                ag(g, j).wait()

        def project_out(c, carry):
            mixed[:, cols(c)] = jnp.dot(
                attended[...], wout[:, cols(c)], preferred_element_type=jnp.float32
            ).astype(jnp.bfloat16)
            ex(c).start()
            return carry

        lax.fori_loop(0, n_out, project_out, 0)
        active = layer_on[s].astype(jnp.float32)

        def finish(c, carry):
            ex(c).wait()
            own = mixed[pl.ds(pl.multiple_of(t * half, BLOCK), half), cols(c)].astype(jnp.float32)
            summed = own + mixed_in[:, cols(c)].astype(jnp.float32)
            base = own_x[k, :, cols(c)].astype(jnp.float32)
            out[k, :, cols(c)] = (base + active * summed).astype(jnp.bfloat16)

            @pl.when((k < BLOCKS - 1) & (s < S - 1))
            def _():
                hand(k, c).start()

            return carry

        lax.fori_loop(0, n_out, finish, 0)
        return carry

    lax.fori_loop(0, BLOCKS, step_body, 0)
    spread(BLOCKS - 1)

    @pl.when(s < S - 1)
    def _():
        for k in range(BLOCKS - 1):
            for c in range(n_out):
                hand(k, c).wait_send()

    def ship_wait(o, carry):
        ship(o).wait()
        return carry

    lax.fori_loop(1, dests, ship_wait, 0)
    own_slots.wait()
    for k in range(BLOCKS):
        for j in range(1, R):
            fx(k, j).wait()


def place_kernel(slots, kind, place, landed, fresh, pool):
    def body(i, carry):
        @pl.when(kind[i] == 0)
        def _():
            pool[i] = jnp.zeros_like(pool[i])

        @pl.when(kind[i] == 1)
        def _():
            pool[i] = landed[place[i]]

        @pl.when(kind[i] == 2)
        def _():
            pool[i] = fresh[place[i]]

        return carry

    lax.fori_loop(0, slots, body, 0)


def local(
    entering,
    arriving,
    w_query,
    w_keyval,
    w_out,
    query_bias,
    keyval_bias,
    norm_gain,
    resident_kv,
    resumed_pages,
    section_active,
    block_table,
):
    R = lax.axis_size("rollout")
    S = lax.axis_size("section")
    r = lax.axis_index("rollout")
    s = lax.axis_index("section")
    width_block, qw = w_query.shape[1:]
    kw = w_keyval.shape[3]
    token_rows = entering.shape[1]
    rows = R * BLOCK
    out_width = w_out.shape[2]
    context = resident_kv.shape[2]
    page_count = block_table.shape[2]
    dests = R * S
    cap = (page_count + dests - 1) // dests
    me = r * S + s

    routing = block_table.reshape(dests, page_count, 2)
    targets = routing[:, :, 0]
    slot_ids = routing[:, :, 1]
    page_ids = jnp.arange(page_count, dtype=jnp.int32)
    before = page_ids[None, :] < page_ids[:, None]
    ranks = jnp.sum(
        ((targets[:, :, None] == targets[:, None, :]) & before[None]).astype(jnp.int32), axis=2
    )
    column = targets[me] * cap + ranks[me]
    buffer_ids = jnp.arange(dests * cap, dtype=jnp.int32)
    source_pages = jnp.minimum(page_ids, context // PAGE - 1)
    pack_pages = jnp.sum(
        jnp.where(buffer_ids[:, None] == column[None, :], source_pages[None, :], 0), axis=1
    ).astype(jnp.int32)
    sources = jnp.arange(dests, dtype=jnp.int32)
    first_of = (resumed_pages[:, None] + (S - 1 - jnp.arange(S, dtype=jnp.int32))[None, :]).reshape(-1)
    switched_on = jnp.broadcast_to(section_active[None, :], (R, S)).reshape(-1) > 0
    turn = page_ids[None, :] - first_of[:, None]
    alive = (turn < BLOCKS) & switched_on[:, None]
    kinds = jnp.where(alive, jnp.where(turn >= 0, 2, 1), 0)
    places = jnp.where(
        kinds == 2,
        jnp.clip(turn, 0, BLOCKS - 1) * dests + sources[:, None],
        sources[:, None] * cap + jnp.minimum(ranks, cap - 1),
    )
    codes = (kinds * (BLOCKS * dests + dests * cap) + places).reshape(-1)
    hit = (targets == me).reshape(-1)[None, :] & (slot_ids.reshape(-1)[None, :] == page_ids[:, None])
    code = jnp.sum(jnp.where(hit, codes[None, :], 0), axis=1).astype(jnp.int32)
    base = BLOCKS * dests + dests * cap
    kind, place = code // base, code % base

    freq = jnp.power(
        jnp.float32(1000000.0), -(jnp.arange(HD // 2, dtype=jnp.float32) * (2.0 / HD))
    )
    freq = jnp.concatenate([freq, freq])[None, :]

    resident = resident_kv[0, 0].reshape(context // PAGE, PAGE, 2 * kw)
    page_shape = (PAGE, 2 * kw)
    bf16 = jnp.bfloat16
    f32 = jnp.float32
    anywhere = pl.BlockSpec(memory_space=pl.ANY)
    vmem = pl.BlockSpec(memory_space=pltpu.VMEM)
    smem = pl.BlockSpec(memory_space=pltpu.SMEM)
    dma = pltpu.SemaphoreType.DMA

    total = -(-(context + BLOCKS * BLOCK) // HD) * HD
    n_rs = (qw + 2 * kw) // CHUNK
    n_out = out_width // CHUNK
    n_kv = kw // HD
    section_out, landed, fresh = pl.pallas_call(
        functools.partial(steps_kernel, (R, S, context)),
        out_shape=(
            jax.ShapeDtypeStruct((BLOCKS, token_rows, out_width), bf16),
            jax.ShapeDtypeStruct((dests, cap) + page_shape, bf16),
            jax.ShapeDtypeStruct((BLOCKS, R, S) + page_shape, bf16),
        ),
        in_specs=[smem] * 3 + [vmem] * 6 + [anywhere] * 4,
        out_specs=(vmem, anywhere, vmem if dests <= 16 else anywhere),
        scratch_shapes=[
            pltpu.VMEM((width_block, qw + 2 * kw), bf16),
            pltpu.VMEM((qw, out_width), bf16),
            pltpu.VMEM((total // PAGE,) + page_shape, bf16),
            pltpu.VMEM((dests, cap) + page_shape, bf16),
            pltpu.VMEM((BLOCKS, token_rows, width_block), bf16),
            pltpu.VMEM((token_rows, width_block), bf16),
            pltpu.VMEM((rows, width_block), bf16),
            pltpu.VMEM((rows, qw + 2 * kw), bf16),
            pltpu.VMEM((rows, HD), f32),
            pltpu.VMEM((rows, qw + 2 * kw), bf16),
            pltpu.VMEM((rows, HD), f32),
            pltpu.VMEM((qw // HD * BLOCK, HD), bf16),
            pltpu.VMEM((rows, qw), bf16),
            pltpu.VMEM((rows, out_width), bf16),
            pltpu.VMEM((token_rows, out_width), bf16),
            dma((4,)),
            dma((n_out,)),
            dma((n_out,)),
            dma((R,)),
            dma((R,)),
            dma((n_rs, R)),
            dma((n_rs, R)),
            dma((n_kv, R)),
            dma((n_kv, R)),
            dma((n_out,)),
            dma((n_out,)),
            dma((BLOCKS, n_out)),
            dma((BLOCKS, n_out)),
            dma((dests,)),
            dma((dests,)),
            dma((BLOCKS, S)),
            dma((BLOCKS, S)),
            dma((BLOCKS, R)),
            dma((BLOCKS, R)),
            dma((BLOCKS + 1,)),
        ],
        compiler_params=pltpu.CompilerParams(
            collective_id=0, has_side_effects=True, vmem_limit_bytes=60 * 1024 * 1024
        ),
        name="relay_steps",
    )(
        resumed_pages,
        section_active,
        pack_pages,
        entering[0],
        arriving,
        norm_gain,
        query_bias,
        keyval_bias.reshape(1, 2 * kw),
        freq,
        w_query[0],
        w_keyval[0].reshape(width_block, 2 * kw),
        w_out[0],
        resident,
    )

    pool = pl.pallas_call(
        functools.partial(place_kernel, page_count),
        out_shape=jax.ShapeDtypeStruct((page_count,) + page_shape, bf16),
        in_specs=[smem, smem, vmem, vmem],
        out_specs=vmem,
        compiler_params=pltpu.CompilerParams(vmem_limit_bytes=48 * 1024 * 1024),
        name="place_pages",
    )(
        kind,
        place,
        landed.reshape((dests * cap,) + page_shape),
        fresh.reshape((BLOCKS * dests,) + page_shape),
    )
    return (section_out[None], pool.reshape(1, 1, page_count, PAGE, 2, kw))


def solution(mesh):
    in_specs = (
        P("section", "tensor", "rollout"),
        P(None, "tensor", "rollout"),
        P("section", "rollout", "tensor"),
        P("section", "rollout", None, "tensor"),
        P("section", "tensor", "rollout"),
        P("section", "tensor"),
        P("section", None, "tensor"),
        P("section", "rollout"),
        P("rollout", "section", None, None, "tensor"),
        P(),
        P(),
        P(),
    )
    out_specs = (
        P("section", None, "tensor", "rollout"),
        P("rollout", "section", None, None, None, "tensor"),
    )
    return jax.shard_map(local, mesh=mesh, in_specs=in_specs, out_specs=out_specs, check_vma=False)
```

```python
import functools
import math

import jax
import jax.numpy as jnp
import numpy as np
from jax import lax
from jax.experimental import pallas as pl
from jax.experimental.pallas import tpu as pltpu
from jax.sharding import PartitionSpec as P

HD = 128
BLOCK = 32
BLOCKS = 3
PAGE = 32
CHUNK = 512
EPS = 1e-06
MESH = pl.DeviceIdType.MESH


def remote(src, dst, send, recv, **where):
    return pltpu.make_async_remote_copy(
        src_ref=src, dst_ref=dst, send_sem=send, recv_sem=recv, device_id=where, device_id_type=MESH
    )


def steps_kernel(
    dims,
    resumed,
    layer_on,
    pack_pages,
    entering,
    arriving,
    gain,
    query_bias,
    keyval_bias,
    freq,
    w_query,
    w_key,
    w_val,
    w_out,
    resident_keys,
    resident_vals,
    out,
    landed,
    fresh,
    wcat,
    wout,
    kv,
    packed,
    own_x,
    peer_x,
    normed,
    part,
    squares,
    part_in,
    squares_in,
    heads,
    attended,
    mixed,
    mixed_in,
    load_sem,
    fwd_s,
    fwd_r,
    sq_s,
    sq_r,
    rs_s,
    rs_r,
    ag_s,
    ag_r,
    ex_s,
    ex_r,
    hand_s,
    hand_r,
    ship_s,
    ship_r,
    fz_s,
    fz_r,
    fx_s,
    fx_r,
    own_sem,
):
    R, S, context = dims
    r = lax.axis_index("rollout")
    s = lax.axis_index("section")
    t = lax.axis_index("tensor")
    other = 1 - t
    token_rows, width = entering.shape
    qw = w_query.shape[1]
    kw = resident_keys.shape[2]
    held = resident_keys.shape[0]
    dests = R * S
    me = r * S + s
    n_rs = wcat.shape[1] // CHUNK
    n_out = wout.shape[1] // CHUNK
    n_kv = kw // HD
    group = qw // kw
    group_width = group * HD
    half = token_rows
    length = (resumed[r] + (S - 1 - s)) * PAGE

    loads = [
        pltpu.make_async_copy(resident_keys, kv.at[pl.ds(0, held), :, pl.ds(0, kw)], load_sem.at[0]),
        pltpu.make_async_copy(resident_vals, kv.at[pl.ds(0, held), :, pl.ds(kw, kw)], load_sem.at[1]),
        pltpu.make_async_copy(w_query, wcat.at[:, pl.ds(0, qw)], load_sem.at[2]),
        pltpu.make_async_copy(w_key, wcat.at[:, pl.ds(qw, kw)], load_sem.at[3]),
        pltpu.make_async_copy(w_val, wcat.at[:, pl.ds(qw + kw, kw)], load_sem.at[4]),
        pltpu.make_async_copy(w_out, wout, load_sem.at[5]),
    ]
    for load in loads:
        load.start()

    barrier = pltpu.get_barrier_semaphore()

    def greet(o, carry):
        d = lax.rem(me + o, dests)
        pl.semaphore_signal(
            barrier, inc=1, device_id={"rollout": d // S, "section": lax.rem(d, S)}, device_id_type=MESH
        )
        return carry

    lax.fori_loop(1, dests, greet, 0)
    pl.semaphore_signal(barrier, inc=1, device_id={"tensor": other}, device_id_type=MESH)

    own_x[0] = entering[...]

    @pl.when(s == 0)
    def _():
        for k in range(1, BLOCKS):
            own_x[k] = arriving[k - 1]

    spare = kv.shape[0] - held
    kv[pl.ds(held, spare)] = jnp.zeros((spare, PAGE, 2 * kw), jnp.bfloat16)
    pl.semaphore_wait(barrier, dests)

    def cols(c, size=CHUNK):
        return pl.ds(pl.multiple_of(c * size, size), size)

    def rows_of(b):
        return pl.ds(pl.multiple_of(b * BLOCK, BLOCK), BLOCK)

    def fwd(k, c):
        return remote(own_x.at[k, :, cols(c)], peer_x.at[:, cols(c)], fwd_s.at[c], fwd_r.at[c], tensor=other)

    def hand(k, c):
        return remote(
            out.at[k, :, cols(c)],
            own_x.at[k + 1, :, cols(c)],
            hand_s.at[k, c],
            hand_r.at[k, c],
            section=jnp.minimum(s + 1, S - 1),
        )

    def ahead(j):
        return lax.rem(r + j, R)

    def behind(j):
        return lax.rem(r + R - j, R)

    def sq(j):
        return remote(
            squares.at[rows_of(ahead(j))], squares_in.at[rows_of(r)], sq_s.at[j], sq_r.at[j], rollout=ahead(j)
        )

    def rs(c, j):
        return remote(
            part.at[rows_of(ahead(j)), cols(c)],
            part_in.at[rows_of(r), cols(c)],
            rs_s.at[c, j],
            rs_r.at[c, j],
            rollout=ahead(j),
        )

    def ag(c, j):
        ref = attended.at[rows_of(r), cols(c, group_width)]
        return remote(ref, ref, ag_s.at[c, j], ag_r.at[c, j], rollout=ahead(j))

    def ex(c):
        return remote(
            mixed.at[pl.ds(pl.multiple_of(other * half, BLOCK), half), cols(c)],
            mixed_in.at[:, cols(c)],
            ex_s.at[c],
            ex_r.at[c],
            tensor=other,
        )

    def ship(o):
        to_r = lax.rem(r + o // S, R)
        to_s = lax.rem(s + lax.rem(o, S), S)
        return remote(
            packed.at[to_r * S + to_s], landed.at[me], ship_s.at[o], ship_r.at[o], rollout=to_r, section=to_s
        )

    def ship_mixed(low, high):
        def one(m, carry):
            ship((m // (S - 1) + 1) * S + lax.rem(m, S - 1) + 1).start()
            return carry

        lax.fori_loop(low, high, one, 0)

    def fz(k, j):
        return remote(
            kv.at[held + k], fresh.at[k, r, s], fz_s.at[k, j], fz_r.at[k, j], section=lax.rem(s + j, S)
        )

    def fx(k, j):
        return remote(fresh.at[k, r], fresh.at[k, r], fx_s.at[k, j], fx_r.at[k, j], rollout=ahead(j))

    def own_page(k):
        return pltpu.make_async_copy(kv.at[held + k], fresh.at[k, r, s], own_sem.at[k])

    own_slots = pltpu.make_async_copy(packed.at[me], landed.at[me], own_sem.at[BLOCKS])

    def spread(k):
        own_page(k).wait()
        for j in range(1, S):
            fz(k, j).wait()
        for j in range(1, R):
            fx(k, j).start()

    mixed_count = (R - 1) * (S - 1)
    loads[0].wait()
    loads[1].wait()

    def pack(d, carry):
        for c in range(packed.shape[1]):
            packed[d, c] = kv[pack_pages[d * packed.shape[1] + c]]
        return carry

    lax.fori_loop(0, dests, pack, 0)
    own_slots.start()
    for o in range(1, S):
        ship(jnp.int32(o)).start()

    def ship_plane(o, carry):
        ship(o * S).start()
        return carry

    lax.fori_loop(1, R, ship_plane, 0)

    def step_body(k, carry):
        for c in range(n_out):
            @pl.when((k > 0) & (s > 0))
            def _(c=c):
                hand(k - 1, c).wait_recv()

            fwd(k, c).start()

        def norm(ref, base):
            def body(i, carry):
                xf = ref[rows_of(i), :].astype(jnp.float32)
                ms = jnp.sum(xf * xf, axis=1, keepdims=True) / width
                rows = pl.ds(pl.multiple_of(base + i * BLOCK, BLOCK), BLOCK)
                normed[rows, :] = (xf * lax.rsqrt(ms + EPS) * gain[...].astype(jnp.float32)).astype(
                    jnp.bfloat16
                )
                squares[rows, :] = jnp.broadcast_to(ms, (BLOCK, HD))
                return carry

            lax.fori_loop(0, half // BLOCK, body, 0)

        norm(own_x.at[k], t * half)
        for c in range(n_out):
            fwd(k, c).wait()
        norm(peer_x, other * half)
        for j in range(1, R):
            sq(j).start()

        @pl.when(k == 0)
        def _():
            for load in loads[2:5]:
                load.wait()

        def project(c, carry):
            part[:, cols(c)] = jnp.dot(
                normed[...], wcat[:, cols(c)], preferred_element_type=jnp.float32
            ).astype(jnp.bfloat16)
            for j in range(1, R):
                rs(c, j).start()
            return carry

        lax.fori_loop(0, n_rs, project, 0)

        @pl.when(k > 0)
        def _():
            spread(k - 1)

        for j in range(1, R):
            sq(j).wait()
        ms = [squares[rows_of(r), :]] + [squares_in[rows_of(behind(j)), :] for j in range(1, R)]
        whole = lax.rsqrt(sum(ms) / R + EPS)
        ratios = []
        for m in ms:
            local = lax.rsqrt(m + EPS)
            ratios.append(jnp.where(local > 0, whole / jnp.where(local > 0, local, 1.0), 0.0)[:, :1])
        angle = (length + k * BLOCK + lax.broadcasted_iota(jnp.int32, (BLOCK, HD), 0)).astype(
            jnp.float32
        ) * freq[...]
        lane = lax.broadcasted_iota(jnp.int32, (BLOCK, HD), 1)
        cos = jnp.cos(angle)
        sin = jnp.sin(angle)
        sin = jnp.where(lane < HD // 2, -sin, sin)

        def rotate(v):
            return v * cos + pltpu.roll(v, HD // 2, 1) * sin

        shifts = keyval_bias[...].astype(jnp.float32)
        for c in range(n_rs):
            for j in range(1, R):
                rs(c, j).wait()
            acc = part[rows_of(r), cols(c)].astype(jnp.float32) * ratios[0]
            for j in range(1, R):
                acc = acc + part_in[rows_of(behind(j)), cols(c)].astype(jnp.float32) * ratios[j]
            low = c * CHUNK
            for h in range(CHUNK // HD):
                at = low + h * HD
                one = acc[:, h * HD : (h + 1) * HD]
                if at < qw:
                    one = rotate(one + query_bias[:, at : at + HD].astype(jnp.float32))
                    heads[at // HD * BLOCK : (at // HD + 1) * BLOCK, :] = one.astype(jnp.bfloat16)
                else:
                    at = at - qw
                    one = one + shifts[at // kw : at // kw + 1, at % kw : at % kw + HD]
                    if at < kw:
                        one = rotate(one)
                    kv[held + k, :, at : at + HD] = one.astype(jnp.bfloat16)
        own_page(k).start()
        for j in range(1, S):
            fz(k, j).start()

        total = kv.shape[0] * PAGE
        column = lax.broadcasted_iota(jnp.int32, (group * BLOCK, total), 1)
        token = lax.rem(lax.broadcasted_iota(jnp.int32, (group * BLOCK, total), 0), BLOCK)
        seen = (column < length) | ((column >= context) & (column - context <= k * BLOCK + token))
        for g in range(n_kv):
            at = g * HD
            scores = lax.dot_general(
                heads[g * group * BLOCK : (g + 1) * group * BLOCK, :],
                kv[:, :, at : at + HD].reshape(total, HD),
                (((1,), (1,)), ((), ())),
                preferred_element_type=jnp.float32,
            )
            scores = jnp.where(seen, scores * (1.0 / math.sqrt(HD)), -1e30)
            powers = jnp.exp(scores - jnp.max(scores, axis=-1, keepdims=True))
            total_power = jnp.sum(powers, axis=-1, keepdims=True)
            got = jnp.dot(
                powers.astype(jnp.bfloat16),
                kv[:, :, kw + at : kw + at + HD].reshape(total, HD),
                preferred_element_type=jnp.float32,
            )
            got = (got / total_power).astype(jnp.bfloat16)
            for i in range(group):
                lane = (g * group + i) * HD
                attended[rows_of(r), lane : lane + HD] = got[i * BLOCK : (i + 1) * BLOCK, :]
            for j in range(1, R):
                ag(g, j).start()

        @pl.when(k == 0)
        def _():
            loads[5].wait()

        @pl.when(k == BLOCKS - 1)
        def _():
            ship_mixed(mixed_count * 7 // 9, mixed_count)
            spread(BLOCKS - 1)

        for g in range(n_kv):
            for j in range(1, R):
                ag(g, j).wait()

        @pl.when(k == 0)
        def _():
            ship_mixed(0, mixed_count * 4 // 9)

        @pl.when(k == 1)
        def _():
            ship_mixed(mixed_count * 4 // 9, mixed_count * 7 // 9)

        def project_out(c, carry):
            mixed[:, cols(c)] = jnp.dot(
                attended[...], wout[:, cols(c)], preferred_element_type=jnp.float32
            ).astype(jnp.bfloat16)
            ex(c).start()
            return carry

        lax.fori_loop(0, n_out, project_out, 0)
        active = layer_on[s].astype(jnp.float32)

        def finish(c, carry):
            ex(c).wait()
            own = mixed[pl.ds(pl.multiple_of(t * half, BLOCK), half), cols(c)].astype(jnp.float32)
            summed = own + mixed_in[:, cols(c)].astype(jnp.float32)
            base = own_x[k, :, cols(c)].astype(jnp.float32)
            out[k, :, cols(c)] = (base + active * summed).astype(jnp.bfloat16)

            @pl.when((k < BLOCKS - 1) & (s < S - 1))
            def _():
                hand(k, c).start()

            return carry

        lax.fori_loop(0, n_out, finish, 0)
        return carry

    lax.fori_loop(0, BLOCKS, step_body, 0)

    @pl.when(s < S - 1)
    def _():
        for k in range(BLOCKS - 1):
            for c in range(n_out):
                hand(k, c).wait_send()

    def ship_wait(o, carry):
        ship(o).wait()
        return carry

    lax.fori_loop(1, dests, ship_wait, 0)
    own_slots.wait()
    for k in range(BLOCKS):
        for j in range(1, R):
            fx(k, j).wait()


def place_kernel(slots, kind, place, landed, fresh, pool):
    def body(i, carry):
        @pl.when(kind[i] == 0)
        def _():
            pool[i] = jnp.zeros_like(pool[i])

        @pl.when(kind[i] == 1)
        def _():
            pool[i] = landed[place[i]]

        @pl.when(kind[i] == 2)
        def _():
            pool[i] = fresh[place[i]]

        return carry

    lax.fori_loop(0, slots, body, 0)


def local(
    entering,
    arriving,
    w_query,
    w_keyval,
    w_out,
    query_bias,
    keyval_bias,
    norm_gain,
    resident_kv,
    resumed_pages,
    section_active,
    block_table,
):
    R = lax.axis_size("rollout")
    S = lax.axis_size("section")
    r = lax.axis_index("rollout")
    s = lax.axis_index("section")
    width_block, qw = w_query.shape[1:]
    kw = w_keyval.shape[3]
    token_rows = entering.shape[1]
    rows = R * BLOCK
    out_width = w_out.shape[2]
    context = resident_kv.shape[2]
    page_count = block_table.shape[2]
    dests = R * S
    cap = (page_count + dests - 1) // dests
    me = r * S + s

    routing = block_table.reshape(dests, page_count, 2)
    targets = routing[:, :, 0]
    slot_ids = routing[:, :, 1]
    page_ids = jnp.arange(page_count, dtype=jnp.int32)
    before = page_ids[None, :] < page_ids[:, None]
    ranks = jnp.sum(
        ((targets[:, :, None] == targets[:, None, :]) & before[None]).astype(jnp.int32), axis=2
    )
    column = targets[me] * cap + ranks[me]
    buffer_ids = jnp.arange(dests * cap, dtype=jnp.int32)
    source_pages = jnp.minimum(page_ids, context // PAGE - 1)
    pack_pages = jnp.sum(
        jnp.where(buffer_ids[:, None] == column[None, :], source_pages[None, :], 0), axis=1
    ).astype(jnp.int32)
    sources = jnp.arange(dests, dtype=jnp.int32)
    first_of = (resumed_pages[:, None] + (S - 1 - jnp.arange(S, dtype=jnp.int32))[None, :]).reshape(-1)
    switched_on = jnp.broadcast_to(section_active[None, :], (R, S)).reshape(-1) > 0
    turn = page_ids[None, :] - first_of[:, None]
    alive = (turn < BLOCKS) & switched_on[:, None]
    kinds = jnp.where(alive, jnp.where(turn >= 0, 2, 1), 0)
    places = jnp.where(
        kinds == 2,
        jnp.clip(turn, 0, BLOCKS - 1) * dests + sources[:, None],
        sources[:, None] * cap + jnp.minimum(ranks, cap - 1),
    )
    codes = (kinds * (BLOCKS * dests + dests * cap) + places).reshape(-1)
    hit = (targets == me).reshape(-1)[None, :] & (slot_ids.reshape(-1)[None, :] == page_ids[:, None])
    code = jnp.sum(jnp.where(hit, codes[None, :], 0), axis=1).astype(jnp.int32)
    base = BLOCKS * dests + dests * cap
    kind, place = code // base, code % base

    freq = np.power(1000000.0, -np.arange(HD // 2) * (2.0 / HD)).astype(np.float32)
    freq = jnp.asarray(np.concatenate([freq, freq])[None, :])

    resident = resident_kv[0, 0].reshape(context // PAGE, PAGE, 2, kw)
    page_shape = (PAGE, 2 * kw)
    bf16 = jnp.bfloat16
    f32 = jnp.float32
    anywhere = pl.BlockSpec(memory_space=pl.ANY)
    vmem = pl.BlockSpec(memory_space=pltpu.VMEM)
    smem = pl.BlockSpec(memory_space=pltpu.SMEM)
    dma = pltpu.SemaphoreType.DMA

    total = -(-(context + BLOCKS * BLOCK) // HD) * HD
    n_rs = (qw + 2 * kw) // CHUNK
    n_out = out_width // CHUNK
    n_kv = kw // HD
    section_out, landed, fresh = pl.pallas_call(
        functools.partial(steps_kernel, (R, S, context)),
        out_shape=(
            jax.ShapeDtypeStruct((BLOCKS, token_rows, out_width), bf16),
            jax.ShapeDtypeStruct((dests, cap) + page_shape, bf16),
            jax.ShapeDtypeStruct((BLOCKS, R, S) + page_shape, bf16),
        ),
        in_specs=[smem] * 3 + [vmem] * 6 + [anywhere] * 6,
        out_specs=(vmem, anywhere, vmem if dests <= 16 else anywhere),
        scratch_shapes=[
            pltpu.VMEM((width_block, qw + 2 * kw), bf16),
            pltpu.VMEM((qw, out_width), bf16),
            pltpu.VMEM((total // PAGE,) + page_shape, bf16),
            pltpu.VMEM((dests, cap) + page_shape, bf16),
            pltpu.VMEM((BLOCKS, token_rows, width_block), bf16),
            pltpu.VMEM((token_rows, width_block), bf16),
            pltpu.VMEM((rows, width_block), bf16),
            pltpu.VMEM((rows, qw + 2 * kw), bf16),
            pltpu.VMEM((rows, HD), f32),
            pltpu.VMEM((rows, qw + 2 * kw), bf16),
            pltpu.VMEM((rows, HD), f32),
            pltpu.VMEM((qw // HD * BLOCK, HD), bf16),
            pltpu.VMEM((rows, qw), bf16),
            pltpu.VMEM((rows, out_width), bf16),
            pltpu.VMEM((token_rows, out_width), bf16),
            dma((6,)),
            dma((n_out,)),
            dma((n_out,)),
            dma((R,)),
            dma((R,)),
            dma((n_rs, R)),
            dma((n_rs, R)),
            dma((n_kv, R)),
            dma((n_kv, R)),
            dma((n_out,)),
            dma((n_out,)),
            dma((BLOCKS, n_out)),
            dma((BLOCKS, n_out)),
            dma((dests,)),
            dma((dests,)),
            dma((BLOCKS, S)),
            dma((BLOCKS, S)),
            dma((BLOCKS, R)),
            dma((BLOCKS, R)),
            dma((BLOCKS + 1,)),
        ],
        compiler_params=pltpu.CompilerParams(
            collective_id=0, has_side_effects=True, vmem_limit_bytes=60 * 1024 * 1024
        ),
        name="relay_steps",
    )(
        resumed_pages,
        section_active,
        pack_pages,
        entering[0],
        arriving,
        norm_gain,
        query_bias,
        keyval_bias[0],
        freq,
        w_query[0],
        w_keyval[0, :, 0],
        w_keyval[0, :, 1],
        w_out[0],
        resident[:, :, 0],
        resident[:, :, 1],
    )

    pool = pl.pallas_call(
        functools.partial(place_kernel, page_count),
        out_shape=jax.ShapeDtypeStruct((page_count,) + page_shape, bf16),
        in_specs=[smem, smem, vmem, vmem],
        out_specs=vmem,
        compiler_params=pltpu.CompilerParams(vmem_limit_bytes=48 * 1024 * 1024),
        name="place_pages",
    )(
        kind,
        place,
        landed.reshape((dests * cap,) + page_shape),
        fresh.reshape((BLOCKS * dests,) + page_shape),
    )
    return (section_out[None], pool.reshape(1, 1, page_count, PAGE, 2, kw))


def solution(mesh):
    in_specs = (
        P("section", "tensor", "rollout"),
        P(None, "tensor", "rollout"),
        P("section", "rollout", "tensor"),
        P("section", "rollout", None, "tensor"),
        P("section", "tensor", "rollout"),
        P("section", "tensor"),
        P("section", None, "tensor"),
        P("section", "rollout"),
        P("rollout", "section", None, None, "tensor"),
        P(),
        P(),
        P(),
    )
    out_specs = (
        P("section", None, "tensor", "rollout"),
        P("rollout", "section", None, None, None, "tensor"),
    )
    return jax.shard_map(local, mesh=mesh, in_specs=in_specs, out_specs=out_specs, check_vma=False)
```

```python
import functools
import math

import jax
import jax.numpy as jnp
import numpy as np
from jax import lax
from jax.experimental import pallas as pl
from jax.experimental.pallas import tpu as pltpu
from jax.sharding import PartitionSpec as P

HD = 128
BLOCK = 32
BLOCKS = 3
PAGE = 32
CHUNK = 512
EPS = 1e-06
MESH = pl.DeviceIdType.MESH


def remote(src, dst, send, recv, **where):
    return pltpu.make_async_remote_copy(
        src_ref=src, dst_ref=dst, send_sem=send, recv_sem=recv, device_id=where, device_id_type=MESH
    )


def steps_kernel(
    dims,
    resumed,
    layer_on,
    pack_pages,
    entering,
    arriving,
    gain,
    query_bias,
    keyval_bias,
    freq,
    w_query,
    w_keyval,
    w_out,
    resident_keys,
    resident_vals,
    out,
    landed,
    fresh,
    wcat,
    wout,
    kv,
    packed,
    own_x,
    peer_x,
    normed,
    part,
    squares,
    part_in,
    squares_in,
    heads,
    attended,
    mixed,
    mixed_in,
    load_sem,
    fwd_s,
    fwd_r,
    sq_s,
    sq_r,
    rs_s,
    rs_r,
    ag_s,
    ag_r,
    ex_s,
    ex_r,
    hand_s,
    hand_r,
    ship_s,
    ship_r,
    fz_s,
    fz_r,
    fx_s,
    fx_r,
    own_sem,
):
    R, S, context = dims
    r = lax.axis_index("rollout")
    s = lax.axis_index("section")
    t = lax.axis_index("tensor")
    other = 1 - t
    token_rows, width = entering.shape
    qw = w_query.shape[1]
    kw = resident_keys.shape[2]
    held = resident_keys.shape[0]
    dests = R * S
    me = r * S + s
    n_rs = wcat.shape[1] // CHUNK
    n_out = wout.shape[1] // CHUNK
    n_kv = kw // HD
    group = qw // kw
    group_width = group * HD
    half = token_rows
    length = (resumed[r] + (S - 1 - s)) * PAGE

    loads = [
        pltpu.make_async_copy(resident_keys, kv.at[pl.ds(0, held), :, pl.ds(0, kw)], load_sem.at[0]),
        pltpu.make_async_copy(resident_vals, kv.at[pl.ds(0, held), :, pl.ds(kw, kw)], load_sem.at[1]),
        pltpu.make_async_copy(w_query, wcat.at[:, pl.ds(0, qw)], load_sem.at[2]),
        pltpu.make_async_copy(w_keyval, wcat.at[:, pl.ds(qw, 2 * kw)], load_sem.at[3]),
        pltpu.make_async_copy(w_out, wout, load_sem.at[4]),
    ]
    for load in loads:
        load.start()

    barrier = pltpu.get_barrier_semaphore()

    def greet(o, carry):
        d = lax.rem(me + o, dests)
        pl.semaphore_signal(
            barrier, inc=1, device_id={"rollout": d // S, "section": lax.rem(d, S)}, device_id_type=MESH
        )
        return carry

    lax.fori_loop(1, dests, greet, 0)
    pl.semaphore_signal(barrier, inc=1, device_id={"tensor": other}, device_id_type=MESH)

    own_x[0] = entering[...]

    @pl.when(s == 0)
    def _():
        for k in range(1, BLOCKS):
            own_x[k] = arriving[k - 1]

    spare = kv.shape[0] - held
    kv[pl.ds(held, spare)] = jnp.zeros((spare, PAGE, 2 * kw), jnp.bfloat16)
    pl.semaphore_wait(barrier, dests)

    def cols(c, size=CHUNK):
        return pl.ds(pl.multiple_of(c * size, size), size)

    def rows_of(b):
        return pl.ds(pl.multiple_of(b * BLOCK, BLOCK), BLOCK)

    def fwd(k, c):
        return remote(own_x.at[k, :, cols(c)], peer_x.at[:, cols(c)], fwd_s.at[c], fwd_r.at[c], tensor=other)

    def hand(k, c):
        return remote(
            out.at[k, :, cols(c)],
            own_x.at[k + 1, :, cols(c)],
            hand_s.at[k, c],
            hand_r.at[k, c],
            section=jnp.minimum(s + 1, S - 1),
        )

    def ahead(j):
        return lax.rem(r + j, R)

    def behind(j):
        return lax.rem(r + R - j, R)

    def sq(j):
        return remote(
            squares.at[rows_of(ahead(j))], squares_in.at[rows_of(r)], sq_s.at[j], sq_r.at[j], rollout=ahead(j)
        )

    def rs(c, j):
        return remote(
            part.at[rows_of(ahead(j)), cols(c)],
            part_in.at[rows_of(r), cols(c)],
            rs_s.at[c, j],
            rs_r.at[c, j],
            rollout=ahead(j),
        )

    def ag(c, j):
        ref = attended.at[rows_of(r), cols(c, group_width)]
        return remote(ref, ref, ag_s.at[c, j], ag_r.at[c, j], rollout=ahead(j))

    def ex(c):
        return remote(
            mixed.at[pl.ds(pl.multiple_of(other * half, BLOCK), half), cols(c)],
            mixed_in.at[:, cols(c)],
            ex_s.at[c],
            ex_r.at[c],
            tensor=other,
        )

    def ship(o):
        to_r = lax.rem(r + o // S, R)
        to_s = lax.rem(s + lax.rem(o, S), S)
        return remote(
            packed.at[to_r * S + to_s], landed.at[me], ship_s.at[o], ship_r.at[o], rollout=to_r, section=to_s
        )

    def ship_mixed(low, high):
        def one(m, carry):
            ship((m // (S - 1) + 1) * S + lax.rem(m, S - 1) + 1).start()
            return carry

        lax.fori_loop(low, high, one, 0)

    def fz(k, j):
        return remote(
            kv.at[held + k], fresh.at[k, r, s], fz_s.at[k, j], fz_r.at[k, j], section=lax.rem(s + j, S)
        )

    def fx(k, j):
        return remote(fresh.at[k, r], fresh.at[k, r], fx_s.at[k, j], fx_r.at[k, j], rollout=ahead(j))

    def own_page(k):
        return pltpu.make_async_copy(kv.at[held + k], fresh.at[k, r, s], own_sem.at[k])

    own_slots = pltpu.make_async_copy(packed.at[me], landed.at[me], own_sem.at[BLOCKS])

    def spread(k):
        own_page(k).wait()
        for j in range(1, S):
            fz(k, j).wait()
        for j in range(1, R):
            fx(k, j).start()

    mixed_count = (R - 1) * (S - 1)
    loads[0].wait()
    loads[1].wait()

    def pack(d, carry):
        for c in range(packed.shape[1]):
            packed[d, c] = kv[pack_pages[d * packed.shape[1] + c]]
        return carry

    lax.fori_loop(0, dests, pack, 0)
    own_slots.start()
    for o in range(1, S):
        ship(jnp.int32(o)).start()

    def ship_plane(o, carry):
        ship(o * S).start()
        return carry

    lax.fori_loop(1, R, ship_plane, 0)

    def step_body(k, carry):
        for c in range(n_out):
            @pl.when((k > 0) & (s > 0))
            def _(c=c):
                hand(k - 1, c).wait_recv()

            fwd(k, c).start()

        def norm(ref, base):
            def body(i, carry):
                xf = ref[rows_of(i), :].astype(jnp.float32)
                ms = jnp.sum(xf * xf, axis=1, keepdims=True) / width
                rows = pl.ds(pl.multiple_of(base + i * BLOCK, BLOCK), BLOCK)
                normed[rows, :] = (xf * lax.rsqrt(ms + EPS) * gain[...].astype(jnp.float32)).astype(
                    jnp.bfloat16
                )
                squares[rows, :] = jnp.broadcast_to(ms, (BLOCK, HD))
                return carry

            lax.fori_loop(0, half // BLOCK, body, 0)

        norm(own_x.at[k], t * half)
        for c in range(n_out):
            fwd(k, c).wait()
        norm(peer_x, other * half)
        for j in range(1, R):
            sq(j).start()

        @pl.when(k == 0)
        def _():
            for load in loads[2:4]:
                load.wait()

        def project(c, carry):
            part[:, cols(c)] = jnp.dot(
                normed[...], wcat[:, cols(c)], preferred_element_type=jnp.float32
            ).astype(jnp.bfloat16)
            for j in range(1, R):
                rs(c, j).start()
            return carry

        lax.fori_loop(0, n_rs, project, 0)

        @pl.when(k > 0)
        def _():
            spread(k - 1)

        for j in range(1, R):
            sq(j).wait()
        ms = [squares[rows_of(r), :]] + [squares_in[rows_of(behind(j)), :] for j in range(1, R)]
        whole = lax.rsqrt(sum(ms) / R + EPS)
        ratios = []
        for m in ms:
            local = lax.rsqrt(m + EPS)
            ratios.append(jnp.where(local > 0, whole / jnp.where(local > 0, local, 1.0), 0.0)[:, :1])
        angle = (length + k * BLOCK + lax.broadcasted_iota(jnp.int32, (BLOCK, HD), 0)).astype(
            jnp.float32
        ) * freq[...]
        lane = lax.broadcasted_iota(jnp.int32, (BLOCK, HD), 1)
        cos = jnp.cos(angle)
        sin = jnp.sin(angle)
        sin = jnp.where(lane < HD // 2, -sin, sin)

        def rotate(v):
            return v * cos + pltpu.roll(v, HD // 2, 1) * sin

        shifts = keyval_bias[...].astype(jnp.float32)
        for c in range(n_rs):
            for j in range(1, R):
                rs(c, j).wait()
            acc = part[rows_of(r), cols(c)].astype(jnp.float32) * ratios[0]
            for j in range(1, R):
                acc = acc + part_in[rows_of(behind(j)), cols(c)].astype(jnp.float32) * ratios[j]
            low = c * CHUNK
            for h in range(CHUNK // HD):
                at = low + h * HD
                one = acc[:, h * HD : (h + 1) * HD]
                if at < qw:
                    one = rotate(one + query_bias[:, at : at + HD].astype(jnp.float32))
                    heads[at // HD * BLOCK : (at // HD + 1) * BLOCK, :] = one.astype(jnp.bfloat16)
                else:
                    at = at - qw
                    one = one + shifts[at // kw : at // kw + 1, at % kw : at % kw + HD]
                    if at < kw:
                        one = rotate(one)
                    kv[held + k, :, at : at + HD] = one.astype(jnp.bfloat16)
        own_page(k).start()
        for j in range(1, S):
            fz(k, j).start()

        total = kv.shape[0] * PAGE
        column = lax.broadcasted_iota(jnp.int32, (group * BLOCK, total), 1)
        token = lax.rem(lax.broadcasted_iota(jnp.int32, (group * BLOCK, total), 0), BLOCK)
        seen = (column < length) | ((column >= context) & (column - context <= k * BLOCK + token))
        scale = math.log2(math.e) / math.sqrt(HD)

        def score(g):
            return lax.dot_general(
                heads[g * group * BLOCK : (g + 1) * group * BLOCK, :],
                kv[:, :, g * HD : (g + 1) * HD].reshape(total, HD),
                (((1,), (1,)), ((), ())),
                preferred_element_type=jnp.float32,
            )

        upcoming = score(0)
        for g in range(n_kv):
            at = g * HD
            scores = jnp.where(seen, upcoming, -1e30)
            if g + 1 < n_kv:
                upcoming = score(g + 1)
            powers = jnp.exp2((scores - jnp.max(scores, axis=-1, keepdims=True)) * scale)
            total_power = jnp.sum(powers, axis=-1, keepdims=True)
            got = jnp.dot(
                powers.astype(jnp.bfloat16),
                kv[:, :, kw + at : kw + at + HD].reshape(total, HD),
                preferred_element_type=jnp.float32,
            )
            got = (got / total_power).astype(jnp.bfloat16)
            for i in range(group):
                lane = (g * group + i) * HD
                attended[rows_of(r), lane : lane + HD] = got[i * BLOCK : (i + 1) * BLOCK, :]
            for j in range(1, R):
                ag(g, j).start()

        @pl.when(k == 0)
        def _():
            loads[4].wait()

        @pl.when(k == BLOCKS - 1)
        def _():
            ship_mixed(mixed_count * 7 // 9, mixed_count)
            spread(BLOCKS - 1)

        for g in range(n_kv):
            for j in range(1, R):
                ag(g, j).wait()

        @pl.when(k == 0)
        def _():
            ship_mixed(0, mixed_count * 4 // 9)

        @pl.when(k == 1)
        def _():
            ship_mixed(mixed_count * 4 // 9, mixed_count * 7 // 9)

        active = layer_on[s].astype(jnp.float32)

        def finish(c):
            ex(c).wait()
            own = mixed[pl.ds(pl.multiple_of(t * half, BLOCK), half), cols(c)].astype(jnp.float32)
            summed = own + mixed_in[:, cols(c)].astype(jnp.float32)
            base = own_x[k, :, cols(c)].astype(jnp.float32)
            out[k, :, cols(c)] = (base + active * summed).astype(jnp.bfloat16)

            @pl.when((k < BLOCKS - 1) & (s < S - 1))
            def _():
                hand(k, c).start()

        def project_out(c, carry):
            mixed[:, cols(c)] = jnp.dot(
                attended[...], wout[:, cols(c)], preferred_element_type=jnp.float32
            ).astype(jnp.bfloat16)
            ex(c).start()

            @pl.when(c > 0)
            def _():
                finish(c - 1)

            return carry

        lax.fori_loop(0, n_out, project_out, 0)
        finish(jnp.int32(n_out - 1))
        return carry

    lax.fori_loop(0, BLOCKS, step_body, 0)

    @pl.when(s < S - 1)
    def _():
        for k in range(BLOCKS - 1):
            for c in range(n_out):
                hand(k, c).wait_send()

    def ship_wait(o, carry):
        ship(o).wait()
        return carry

    lax.fori_loop(1, dests, ship_wait, 0)
    own_slots.wait()
    for k in range(BLOCKS):
        for j in range(1, R):
            fx(k, j).wait()


def place_kernel(slots, kind, place, landed, fresh, pool):
    def body(i, carry):
        @pl.when(kind[i] == 0)
        def _():
            pool[i] = jnp.zeros_like(pool[i])

        @pl.when(kind[i] == 1)
        def _():
            pool[i] = landed[place[i]]

        @pl.when(kind[i] == 2)
        def _():
            pool[i] = fresh[place[i]]

        return carry

    lax.fori_loop(0, slots, body, 0)


def local(
    entering,
    arriving,
    w_query,
    w_keyval,
    w_out,
    query_bias,
    keyval_bias,
    norm_gain,
    resident_kv,
    resumed_pages,
    section_active,
    block_table,
):
    R = lax.axis_size("rollout")
    S = lax.axis_size("section")
    r = lax.axis_index("rollout")
    s = lax.axis_index("section")
    width_block, qw = w_query.shape[1:]
    kw = w_keyval.shape[3]
    token_rows = entering.shape[1]
    rows = R * BLOCK
    out_width = w_out.shape[2]
    context = resident_kv.shape[2]
    page_count = block_table.shape[2]
    dests = R * S
    cap = (page_count + dests - 1) // dests
    me = r * S + s

    routing = block_table.reshape(dests, page_count, 2)
    targets = routing[:, :, 0]
    slot_ids = routing[:, :, 1]
    page_ids = jnp.arange(page_count, dtype=jnp.int32)
    before = page_ids[None, :] < page_ids[:, None]
    ranks = jnp.sum(
        ((targets[:, :, None] == targets[:, None, :]) & before[None]).astype(jnp.int32), axis=2
    )
    column = targets[me] * cap + ranks[me]
    buffer_ids = jnp.arange(dests * cap, dtype=jnp.int32)
    source_pages = jnp.minimum(page_ids, context // PAGE - 1)
    pack_pages = jnp.sum(
        jnp.where(buffer_ids[:, None] == column[None, :], source_pages[None, :], 0), axis=1
    ).astype(jnp.int32)
    sources = jnp.arange(dests, dtype=jnp.int32)
    first_of = (resumed_pages[:, None] + (S - 1 - jnp.arange(S, dtype=jnp.int32))[None, :]).reshape(-1)
    switched_on = jnp.broadcast_to(section_active[None, :], (R, S)).reshape(-1) > 0
    turn = page_ids[None, :] - first_of[:, None]
    alive = (turn < BLOCKS) & switched_on[:, None]
    kinds = jnp.where(alive, jnp.where(turn >= 0, 2, 1), 0)
    places = jnp.where(
        kinds == 2,
        jnp.clip(turn, 0, BLOCKS - 1) * dests + sources[:, None],
        sources[:, None] * cap + jnp.minimum(ranks, cap - 1),
    )
    codes = (kinds * (BLOCKS * dests + dests * cap) + places).reshape(-1)
    hit = (targets == me).reshape(-1)[None, :] & (slot_ids.reshape(-1)[None, :] == page_ids[:, None])
    code = jnp.sum(jnp.where(hit, codes[None, :], 0), axis=1).astype(jnp.int32)
    base = BLOCKS * dests + dests * cap
    kind, place = code // base, code % base

    freq = np.power(1000000.0, -np.arange(HD // 2) * (2.0 / HD)).astype(np.float32)
    freq = jnp.asarray(np.concatenate([freq, freq])[None, :])

    resident = resident_kv[0, 0].reshape(context // PAGE, PAGE, 2, kw)
    page_shape = (PAGE, 2 * kw)
    bf16 = jnp.bfloat16
    f32 = jnp.float32
    anywhere = pl.BlockSpec(memory_space=pl.ANY)
    vmem = pl.BlockSpec(memory_space=pltpu.VMEM)
    smem = pl.BlockSpec(memory_space=pltpu.SMEM)
    dma = pltpu.SemaphoreType.DMA

    total = -(-(context + BLOCKS * BLOCK) // HD) * HD
    n_rs = (qw + 2 * kw) // CHUNK
    n_out = out_width // CHUNK
    n_kv = kw // HD
    section_out, landed, fresh = pl.pallas_call(
        functools.partial(steps_kernel, (R, S, context)),
        out_shape=(
            jax.ShapeDtypeStruct((BLOCKS, token_rows, out_width), bf16),
            jax.ShapeDtypeStruct((dests, cap) + page_shape, bf16),
            jax.ShapeDtypeStruct((BLOCKS, R, S) + page_shape, bf16),
        ),
        in_specs=[smem] * 3 + [vmem] * 6 + [anywhere] * 5,
        out_specs=(vmem, anywhere, vmem if dests <= 16 else anywhere),
        scratch_shapes=[
            pltpu.VMEM((width_block, qw + 2 * kw), bf16),
            pltpu.VMEM((qw, out_width), bf16),
            pltpu.VMEM((total // PAGE,) + page_shape, bf16),
            pltpu.VMEM((dests, cap) + page_shape, bf16),
            pltpu.VMEM((BLOCKS, token_rows, width_block), bf16),
            pltpu.VMEM((token_rows, width_block), bf16),
            pltpu.VMEM((rows, width_block), bf16),
            pltpu.VMEM((rows, qw + 2 * kw), bf16),
            pltpu.VMEM((rows, HD), f32),
            pltpu.VMEM((rows, qw + 2 * kw), bf16),
            pltpu.VMEM((rows, HD), f32),
            pltpu.VMEM((qw // HD * BLOCK, HD), bf16),
            pltpu.VMEM((rows, qw), bf16),
            pltpu.VMEM((rows, out_width), bf16),
            pltpu.VMEM((token_rows, out_width), bf16),
            dma((5,)),
            dma((n_out,)),
            dma((n_out,)),
            dma((R,)),
            dma((R,)),
            dma((n_rs, R)),
            dma((n_rs, R)),
            dma((n_kv, R)),
            dma((n_kv, R)),
            dma((n_out,)),
            dma((n_out,)),
            dma((BLOCKS, n_out)),
            dma((BLOCKS, n_out)),
            dma((dests,)),
            dma((dests,)),
            dma((BLOCKS, S)),
            dma((BLOCKS, S)),
            dma((BLOCKS, R)),
            dma((BLOCKS, R)),
            dma((BLOCKS + 1,)),
        ],
        compiler_params=pltpu.CompilerParams(
            collective_id=0, has_side_effects=True, vmem_limit_bytes=60 * 1024 * 1024
        ),
        name="relay_steps",
    )(
        resumed_pages,
        section_active,
        pack_pages,
        entering[0],
        arriving,
        norm_gain,
        query_bias,
        keyval_bias[0],
        freq,
        w_query[0],
        w_keyval[0].reshape(width_block, 2 * kw),
        w_out[0],
        resident[:, :, 0],
        resident[:, :, 1],
    )

    pool = pl.pallas_call(
        functools.partial(place_kernel, page_count),
        out_shape=jax.ShapeDtypeStruct((page_count,) + page_shape, bf16),
        in_specs=[smem, smem, vmem, vmem],
        out_specs=vmem,
        compiler_params=pltpu.CompilerParams(vmem_limit_bytes=48 * 1024 * 1024),
        name="place_pages",
    )(
        kind,
        place,
        landed.reshape((dests * cap,) + page_shape),
        fresh.reshape((BLOCKS * dests,) + page_shape),
    )
    return (section_out[None], pool.reshape(1, 1, page_count, PAGE, 2, kw))


def solution(mesh):
    in_specs = (
        P("section", "tensor", "rollout"),
        P(None, "tensor", "rollout"),
        P("section", "rollout", "tensor"),
        P("section", "rollout", None, "tensor"),
        P("section", "tensor", "rollout"),
        P("section", "tensor"),
        P("section", None, "tensor"),
        P("section", "rollout"),
        P("rollout", "section", None, None, "tensor"),
        P(),
        P(),
        P(),
    )
    out_specs = (
        P("section", None, "tensor", "rollout"),
        P("rollout", "section", None, None, None, "tensor"),
    )
    return jax.shard_map(local, mesh=mesh, in_specs=in_specs, out_specs=out_specs, check_vma=False)
```

```python
import functools
import math

import jax
import jax.numpy as jnp
import numpy as np
from jax import lax
from jax.experimental import pallas as pl
from jax.experimental.pallas import tpu as pltpu
from jax.sharding import PartitionSpec as P

HD = 128
BLOCK = 32
BLOCKS = 3
PAGE = 32
CHUNK = 512
EPS = 1e-06
MESH = pl.DeviceIdType.MESH


def remote(src, dst, send, recv, **where):
    return pltpu.make_async_remote_copy(
        src_ref=src, dst_ref=dst, send_sem=send, recv_sem=recv, device_id=where, device_id_type=MESH
    )


def steps_kernel(
    dims,
    resumed,
    layer_on,
    pack_pages,
    entering,
    arriving,
    gain,
    query_bias,
    keyval_bias,
    freq,
    w_query,
    w_keyval,
    w_out,
    resident_keys,
    resident_vals,
    out,
    landed,
    fresh,
    wcat,
    wout,
    kv,
    packed,
    own_x,
    peer_x,
    normed,
    part,
    squares,
    part_in,
    squares_in,
    heads,
    attended,
    mixed,
    mixed_in,
    load_sem,
    fwd_s,
    fwd_r,
    sq_s,
    sq_r,
    rs_s,
    rs_r,
    ag_s,
    ag_r,
    ex_s,
    ex_r,
    hand_s,
    hand_r,
    ship_s,
    ship_r,
    fz_s,
    fz_r,
    fx_s,
    fx_r,
    own_sem,
):
    R, S, context = dims
    r = lax.axis_index("rollout")
    s = lax.axis_index("section")
    t = lax.axis_index("tensor")
    other = 1 - t
    token_rows, width = entering.shape
    qw = w_query.shape[1]
    kw = resident_keys.shape[2]
    held = resident_keys.shape[0]
    dests = R * S
    me = r * S + s
    n_rs = wcat.shape[1] // CHUNK
    n_out = wout.shape[1] // CHUNK
    n_kv = kw // HD
    group = qw // kw
    group_width = group * HD
    half = token_rows
    length = (resumed[r] + (S - 1 - s)) * PAGE

    loads = [
        pltpu.make_async_copy(resident_keys, kv.at[pl.ds(0, held), :, pl.ds(0, kw)], load_sem.at[0]),
        pltpu.make_async_copy(resident_vals, kv.at[pl.ds(0, held), :, pl.ds(kw, kw)], load_sem.at[1]),
        pltpu.make_async_copy(w_query, wcat.at[:, pl.ds(0, qw)], load_sem.at[2]),
        pltpu.make_async_copy(w_keyval, wcat.at[:, pl.ds(qw, 2 * kw)], load_sem.at[3]),
        pltpu.make_async_copy(w_out, wout, load_sem.at[4]),
    ]
    for load in loads:
        load.start()

    barrier = pltpu.get_barrier_semaphore()

    def greet(o, carry):
        d = lax.rem(me + o, dests)
        pl.semaphore_signal(
            barrier, inc=1, device_id={"rollout": d // S, "section": lax.rem(d, S)}, device_id_type=MESH
        )
        return carry

    lax.fori_loop(1, dests, greet, 0)
    pl.semaphore_signal(barrier, inc=1, device_id={"tensor": other}, device_id_type=MESH)

    own_x[0] = entering[...]

    @pl.when(s == 0)
    def _():
        for k in range(1, BLOCKS):
            own_x[k] = arriving[k - 1]

    spare = kv.shape[0] - held
    kv[pl.ds(held, spare)] = jnp.zeros((spare, PAGE, 2 * kw), jnp.bfloat16)
    pl.semaphore_wait(barrier, dests)

    def cols(c, size=CHUNK):
        return pl.ds(pl.multiple_of(c * size, size), size)

    def rows_of(b):
        return pl.ds(pl.multiple_of(b * BLOCK, BLOCK), BLOCK)

    def fwd(k, c):
        return remote(own_x.at[k, :, cols(c)], peer_x.at[:, cols(c)], fwd_s.at[c], fwd_r.at[c], tensor=other)

    def hand(k, c):
        return remote(
            out.at[k, :, cols(c)],
            own_x.at[k + 1, :, cols(c)],
            hand_s.at[k, c],
            hand_r.at[k, c],
            section=jnp.minimum(s + 1, S - 1),
        )

    def ahead(j):
        return lax.rem(r + j, R)

    def behind(j):
        return lax.rem(r + R - j, R)

    def sq(j):
        return remote(
            squares.at[rows_of(ahead(j))], squares_in.at[rows_of(r)], sq_s.at[j], sq_r.at[j], rollout=ahead(j)
        )

    def rs(c, j):
        return remote(
            part.at[rows_of(ahead(j)), cols(c)],
            part_in.at[rows_of(r), cols(c)],
            rs_s.at[c, j],
            rs_r.at[c, j],
            rollout=ahead(j),
        )

    def ag(c, j):
        ref = attended.at[rows_of(r), cols(c, group_width)]
        return remote(ref, ref, ag_s.at[c, j], ag_r.at[c, j], rollout=ahead(j))

    def ex(c):
        return remote(
            mixed.at[pl.ds(pl.multiple_of(other * half, BLOCK), half), cols(c)],
            mixed_in.at[:, cols(c)],
            ex_s.at[c],
            ex_r.at[c],
            tensor=other,
        )

    def ship(o):
        to_r = lax.rem(r + o // S, R)
        to_s = lax.rem(s + lax.rem(o, S), S)
        return remote(
            packed.at[to_r * S + to_s], landed.at[me], ship_s.at[o], ship_r.at[o], rollout=to_r, section=to_s
        )

    def ship_mixed(low, high):
        def one(m, carry):
            ship((m // (S - 1) + 1) * S + lax.rem(m, S - 1) + 1).start()
            return carry

        lax.fori_loop(low, high, one, 0)

    def fz(k, j):
        return remote(
            kv.at[held + k], fresh.at[k, r, s], fz_s.at[k, j], fz_r.at[k, j], section=lax.rem(s + j, S)
        )

    def fx(k, j):
        return remote(fresh.at[k, r], fresh.at[k, r], fx_s.at[k, j], fx_r.at[k, j], rollout=ahead(j))

    def own_page(k):
        return pltpu.make_async_copy(kv.at[held + k], fresh.at[k, r, s], own_sem.at[k])

    own_slots = pltpu.make_async_copy(packed.at[me], landed.at[me], own_sem.at[BLOCKS])

    def spread(k):
        own_page(k).wait()
        for j in range(1, S):
            fz(k, j).wait()
        for j in range(1, R):
            fx(k, j).start()

    mixed_count = (R - 1) * (S - 1)
    loads[0].wait()
    loads[1].wait()

    def pack(d, carry):
        for c in range(packed.shape[1]):
            packed[d, c] = kv[pack_pages[d * packed.shape[1] + c]]
        return carry

    lax.fori_loop(0, dests, pack, 0)
    own_slots.start()
    for o in range(1, S):
        ship(jnp.int32(o)).start()

    def ship_plane(o, carry):
        ship(o * S).start()
        return carry

    lax.fori_loop(1, R, ship_plane, 0)

    def step_body(k, carry):
        for c in range(n_out):
            @pl.when((k > 0) & (s > 0))
            def _(c=c):
                hand(k - 1, c).wait_recv()

            fwd(k, c).start()

        def norm(ref, base):
            def body(i, carry):
                xf = ref[rows_of(i), :].astype(jnp.float32)
                ms = jnp.sum(xf * xf, axis=1, keepdims=True) / width
                rows = pl.ds(pl.multiple_of(base + i * BLOCK, BLOCK), BLOCK)
                normed[rows, :] = (xf * lax.rsqrt(ms + EPS) * gain[...].astype(jnp.float32)).astype(
                    jnp.bfloat16
                )
                squares[rows, :] = jnp.broadcast_to(ms, (BLOCK, HD))
                return carry

            lax.fori_loop(0, half // BLOCK, body, 0)

        norm(own_x.at[k], t * half)
        for c in range(n_out):
            fwd(k, c).wait()
        norm(peer_x, other * half)
        for j in range(1, R):
            sq(j).start()

        @pl.when(k == 0)
        def _():
            for load in loads[2:4]:
                load.wait()

        def project(c, carry):
            part[:, cols(c)] = jnp.dot(
                normed[...], wcat[:, cols(c)], preferred_element_type=jnp.float32
            ).astype(jnp.bfloat16)
            for j in range(1, R):
                rs(c, j).start()
            return carry

        lax.fori_loop(0, n_rs, project, 0)

        @pl.when(k == 1)
        def _():
            ship_mixed(mixed_count * 2 // 9, mixed_count * 4 // 9)

        @pl.when(k == 2)
        def _():
            ship_mixed(mixed_count * 7 // 9, mixed_count)

        for j in range(1, R):
            sq(j).wait()
        ms = [squares[rows_of(r), :]] + [squares_in[rows_of(behind(j)), :] for j in range(1, R)]
        whole = lax.rsqrt(sum(ms) / R + EPS)
        ratios = []
        for m in ms:
            local = lax.rsqrt(m + EPS)
            ratios.append(jnp.where(local > 0, whole / jnp.where(local > 0, local, 1.0), 0.0)[:, :1])
        angle = (length + k * BLOCK + lax.broadcasted_iota(jnp.int32, (BLOCK, HD), 0)).astype(
            jnp.float32
        ) * freq[...]
        lane = lax.broadcasted_iota(jnp.int32, (BLOCK, HD), 1)
        cos = jnp.cos(angle)
        sin = jnp.sin(angle)
        sin = jnp.where(lane < HD // 2, -sin, sin)

        def rotate(v):
            return v * cos + pltpu.roll(v, HD // 2, 1) * sin

        shifts = keyval_bias[...].astype(jnp.float32)
        for c in range(n_rs):
            for j in range(1, R):
                rs(c, j).wait()
            acc = part[rows_of(r), cols(c)].astype(jnp.float32) * ratios[0]
            for j in range(1, R):
                acc = acc + part_in[rows_of(behind(j)), cols(c)].astype(jnp.float32) * ratios[j]
            low = c * CHUNK
            for h in range(CHUNK // HD):
                at = low + h * HD
                one = acc[:, h * HD : (h + 1) * HD]
                if at < qw:
                    one = rotate(one + query_bias[:, at : at + HD].astype(jnp.float32))
                    heads[at // HD * BLOCK : (at // HD + 1) * BLOCK, :] = one.astype(jnp.bfloat16)
                else:
                    at = at - qw
                    one = one + shifts[at // kw : at // kw + 1, at % kw : at % kw + HD]
                    if at < kw:
                        one = rotate(one)
                    kv[held + k, :, at : at + HD] = one.astype(jnp.bfloat16)
        own_page(k).start()
        for j in range(1, S):
            fz(k, j).start()

        total = kv.shape[0] * PAGE
        column = lax.broadcasted_iota(jnp.int32, (group * BLOCK, total), 1)
        token = lax.rem(lax.broadcasted_iota(jnp.int32, (group * BLOCK, total), 0), BLOCK)
        seen = (column < length) | ((column >= context) & (column - context <= k * BLOCK + token))
        scale = math.log2(math.e) / math.sqrt(HD)

        def score(g):
            return lax.dot_general(
                heads[g * group * BLOCK : (g + 1) * group * BLOCK, :],
                kv[:, :, g * HD : (g + 1) * HD].reshape(total, HD),
                (((1,), (1,)), ((), ())),
                preferred_element_type=jnp.float32,
            )

        upcoming = score(0)
        for g in range(n_kv):
            at = g * HD
            scores = jnp.where(seen, upcoming, -1e30)
            if g + 1 < n_kv:
                upcoming = score(g + 1)
            powers = jnp.exp2((scores - jnp.max(scores, axis=-1, keepdims=True)) * scale)
            total_power = jnp.sum(powers, axis=-1, keepdims=True)
            got = jnp.dot(
                powers.astype(jnp.bfloat16),
                kv[:, :, kw + at : kw + at + HD].reshape(total, HD),
                preferred_element_type=jnp.float32,
            )
            got = (got / total_power).astype(jnp.bfloat16)
            for i in range(group):
                lane = (g * group + i) * HD
                attended[rows_of(r), lane : lane + HD] = got[i * BLOCK : (i + 1) * BLOCK, :]
            for j in range(1, R):
                ag(g, j).start()

        @pl.when(k == 0)
        def _():
            loads[4].wait()

        @pl.when(k == BLOCKS - 1)
        def _():
            spread(BLOCKS - 1)

        for g in range(n_kv):
            for j in range(1, R):
                ag(g, j).wait()

        active = layer_on[s].astype(jnp.float32)

        def finish(c):
            ex(c).wait()
            own = mixed[pl.ds(pl.multiple_of(t * half, BLOCK), half), cols(c)].astype(jnp.float32)
            summed = own + mixed_in[:, cols(c)].astype(jnp.float32)
            base = own_x[k, :, cols(c)].astype(jnp.float32)
            out[k, :, cols(c)] = (base + active * summed).astype(jnp.bfloat16)

            @pl.when((k < BLOCKS - 1) & (s < S - 1))
            def _():
                hand(k, c).start()

        def project_out(c, carry):
            mixed[:, cols(c)] = jnp.dot(
                attended[...], wout[:, cols(c)], preferred_element_type=jnp.float32
            ).astype(jnp.bfloat16)
            ex(c).start()

            @pl.when(c > 0)
            def _():
                finish(c - 1)

            return carry

        lax.fori_loop(0, n_out, project_out, 0)
        finish(jnp.int32(n_out - 1))

        @pl.when(k < BLOCKS - 1)
        def _():
            spread(k)

        @pl.when(k == 0)
        def _():
            ship_mixed(0, mixed_count * 2 // 9)

        @pl.when(k == 1)
        def _():
            ship_mixed(mixed_count * 4 // 9, mixed_count * 7 // 9)

        return carry

    lax.fori_loop(0, BLOCKS, step_body, 0)

    @pl.when(s < S - 1)
    def _():
        for k in range(BLOCKS - 1):
            for c in range(n_out):
                hand(k, c).wait_send()

    def ship_wait(o, carry):
        ship(o).wait()
        return carry

    lax.fori_loop(1, dests, ship_wait, 0)
    own_slots.wait()
    for k in range(BLOCKS):
        for j in range(1, R):
            fx(k, j).wait()


def place_kernel(slots, kind, place, landed, fresh, pool):
    def body(i, carry):
        @pl.when(kind[i] == 0)
        def _():
            pool[i] = jnp.zeros_like(pool[i])

        @pl.when(kind[i] == 1)
        def _():
            pool[i] = landed[place[i]]

        @pl.when(kind[i] == 2)
        def _():
            pool[i] = fresh[place[i]]

        return carry

    lax.fori_loop(0, slots, body, 0)


def local(
    entering,
    arriving,
    w_query,
    w_keyval,
    w_out,
    query_bias,
    keyval_bias,
    norm_gain,
    resident_kv,
    resumed_pages,
    section_active,
    block_table,
):
    R = lax.axis_size("rollout")
    S = lax.axis_size("section")
    r = lax.axis_index("rollout")
    s = lax.axis_index("section")
    width_block, qw = w_query.shape[1:]
    kw = w_keyval.shape[3]
    token_rows = entering.shape[1]
    rows = R * BLOCK
    out_width = w_out.shape[2]
    context = resident_kv.shape[2]
    page_count = block_table.shape[2]
    dests = R * S
    cap = (page_count + dests - 1) // dests
    me = r * S + s

    routing = block_table.reshape(dests, page_count, 2)
    targets = routing[:, :, 0]
    slot_ids = routing[:, :, 1]
    page_ids = jnp.arange(page_count, dtype=jnp.int32)
    before = page_ids[None, :] < page_ids[:, None]
    ranks = jnp.sum(
        ((targets[:, :, None] == targets[:, None, :]) & before[None]).astype(jnp.int32), axis=2
    )
    column = targets[me] * cap + ranks[me]
    buffer_ids = jnp.arange(dests * cap, dtype=jnp.int32)
    source_pages = jnp.minimum(page_ids, context // PAGE - 1)
    pack_pages = jnp.sum(
        jnp.where(buffer_ids[:, None] == column[None, :], source_pages[None, :], 0), axis=1
    ).astype(jnp.int32)
    sources = jnp.arange(dests, dtype=jnp.int32)
    first_of = (resumed_pages[:, None] + (S - 1 - jnp.arange(S, dtype=jnp.int32))[None, :]).reshape(-1)
    switched_on = jnp.broadcast_to(section_active[None, :], (R, S)).reshape(-1) > 0
    turn = page_ids[None, :] - first_of[:, None]
    alive = (turn < BLOCKS) & switched_on[:, None]
    kinds = jnp.where(alive, jnp.where(turn >= 0, 2, 1), 0)
    places = jnp.where(
        kinds == 2,
        jnp.clip(turn, 0, BLOCKS - 1) * dests + sources[:, None],
        sources[:, None] * cap + jnp.minimum(ranks, cap - 1),
    )
    codes = (kinds * (BLOCKS * dests + dests * cap) + places).reshape(-1)
    hit = (targets == me).reshape(-1)[None, :] & (slot_ids.reshape(-1)[None, :] == page_ids[:, None])
    code = jnp.sum(jnp.where(hit, codes[None, :], 0), axis=1).astype(jnp.int32)
    base = BLOCKS * dests + dests * cap
    kind, place = code // base, code % base

    freq = np.power(1000000.0, -np.arange(HD // 2) * (2.0 / HD)).astype(np.float32)
    freq = jnp.asarray(np.concatenate([freq, freq])[None, :])

    resident = resident_kv[0, 0].reshape(context // PAGE, PAGE, 2, kw)
    page_shape = (PAGE, 2 * kw)
    bf16 = jnp.bfloat16
    f32 = jnp.float32
    anywhere = pl.BlockSpec(memory_space=pl.ANY)
    vmem = pl.BlockSpec(memory_space=pltpu.VMEM)
    smem = pl.BlockSpec(memory_space=pltpu.SMEM)
    dma = pltpu.SemaphoreType.DMA

    total = -(-(context + BLOCKS * BLOCK) // HD) * HD
    n_rs = (qw + 2 * kw) // CHUNK
    n_out = out_width // CHUNK
    n_kv = kw // HD
    section_out, landed, fresh = pl.pallas_call(
        functools.partial(steps_kernel, (R, S, context)),
        out_shape=(
            jax.ShapeDtypeStruct((BLOCKS, token_rows, out_width), bf16),
            jax.ShapeDtypeStruct((dests, cap) + page_shape, bf16),
            jax.ShapeDtypeStruct((BLOCKS, R, S) + page_shape, bf16),
        ),
        in_specs=[smem] * 3 + [vmem] * 6 + [anywhere] * 5,
        out_specs=(vmem, anywhere, vmem if dests <= 16 else anywhere),
        scratch_shapes=[
            pltpu.VMEM((width_block, qw + 2 * kw), bf16),
            pltpu.VMEM((qw, out_width), bf16),
            pltpu.VMEM((total // PAGE,) + page_shape, bf16),
            pltpu.VMEM((dests, cap) + page_shape, bf16),
            pltpu.VMEM((BLOCKS, token_rows, width_block), bf16),
            pltpu.VMEM((token_rows, width_block), bf16),
            pltpu.VMEM((rows, width_block), bf16),
            pltpu.VMEM((rows, qw + 2 * kw), bf16),
            pltpu.VMEM((rows, HD), f32),
            pltpu.VMEM((rows, qw + 2 * kw), bf16),
            pltpu.VMEM((rows, HD), f32),
            pltpu.VMEM((qw // HD * BLOCK, HD), bf16),
            pltpu.VMEM((rows, qw), bf16),
            pltpu.VMEM((rows, out_width), bf16),
            pltpu.VMEM((token_rows, out_width), bf16),
            dma((5,)),
            dma((n_out,)),
            dma((n_out,)),
            dma((R,)),
            dma((R,)),
            dma((n_rs, R)),
            dma((n_rs, R)),
            dma((n_kv, R)),
            dma((n_kv, R)),
            dma((n_out,)),
            dma((n_out,)),
            dma((BLOCKS, n_out)),
            dma((BLOCKS, n_out)),
            dma((dests,)),
            dma((dests,)),
            dma((BLOCKS, S)),
            dma((BLOCKS, S)),
            dma((BLOCKS, R)),
            dma((BLOCKS, R)),
            dma((BLOCKS + 1,)),
        ],
        compiler_params=pltpu.CompilerParams(
            collective_id=0, has_side_effects=True, vmem_limit_bytes=60 * 1024 * 1024
        ),
        name="relay_steps",
    )(
        resumed_pages,
        section_active,
        pack_pages,
        entering[0],
        arriving,
        norm_gain,
        query_bias,
        keyval_bias[0],
        freq,
        w_query[0],
        w_keyval[0].reshape(width_block, 2 * kw),
        w_out[0],
        resident[:, :, 0],
        resident[:, :, 1],
    )

    pool = pl.pallas_call(
        functools.partial(place_kernel, page_count),
        out_shape=jax.ShapeDtypeStruct((page_count,) + page_shape, bf16),
        in_specs=[smem, smem, vmem, vmem],
        out_specs=vmem,
        compiler_params=pltpu.CompilerParams(vmem_limit_bytes=48 * 1024 * 1024),
        name="place_pages",
    )(
        kind,
        place,
        landed.reshape((dests * cap,) + page_shape),
        fresh.reshape((BLOCKS * dests,) + page_shape),
    )
    return (section_out[None], pool.reshape(1, 1, page_count, PAGE, 2, kw))


def solution(mesh):
    in_specs = (
        P("section", "tensor", "rollout"),
        P(None, "tensor", "rollout"),
        P("section", "rollout", "tensor"),
        P("section", "rollout", None, "tensor"),
        P("section", "tensor", "rollout"),
        P("section", "tensor"),
        P("section", None, "tensor"),
        P("section", "rollout"),
        P("rollout", "section", None, None, "tensor"),
        P(),
        P(),
        P(),
    )
    out_specs = (
        P("section", None, "tensor", "rollout"),
        P("rollout", "section", None, None, None, "tensor"),
    )
    return jax.shard_map(local, mesh=mesh, in_specs=in_specs, out_specs=out_specs, check_vma=False)
```

```python
import functools
import math

import jax
import jax.numpy as jnp
import numpy as np
from jax import lax
from jax.experimental import pallas as pl
from jax.experimental.pallas import tpu as pltpu
from jax.sharding import PartitionSpec as P

HD = 128
BLOCK = 32
BLOCKS = 3
PAGE = 32
CHUNK = 512
EPS = 1e-06
MESH = pl.DeviceIdType.MESH


def remote(src, dst, send, recv, **where):
    return pltpu.make_async_remote_copy(
        src_ref=src, dst_ref=dst, send_sem=send, recv_sem=recv, device_id=where, device_id_type=MESH
    )


def steps_kernel(
    dims,
    resumed,
    layer_on,
    pack_pages,
    entering,
    arriving,
    gain,
    query_bias,
    keyval_bias,
    freq,
    w_query,
    w_keyval,
    w_out,
    resident_keys,
    resident_vals,
    out,
    landed,
    fresh,
    wcat,
    wout,
    kv,
    packed,
    own_x,
    peer_x,
    normed,
    part,
    squares,
    part_in,
    squares_in,
    heads,
    attended,
    mixed,
    mixed_in,
    load_sem,
    fwd_s,
    fwd_r,
    sq_s,
    sq_r,
    rs_s,
    rs_r,
    ag_s,
    ag_r,
    ex_s,
    ex_r,
    hand_s,
    hand_r,
    ship_s,
    ship_r,
    fz_s,
    fz_r,
    fx_s,
    fx_r,
    own_sem,
):
    R, S, context = dims
    r = lax.axis_index("rollout")
    s = lax.axis_index("section")
    t = lax.axis_index("tensor")
    other = 1 - t
    token_rows, width = entering.shape
    qw = w_query.shape[1]
    kw = resident_keys.shape[2]
    held = resident_keys.shape[0]
    dests = R * S
    me = r * S + s
    n_rs = wcat.shape[1] // CHUNK
    n_out = wout.shape[1] // CHUNK
    n_kv = kw // HD
    group = qw // kw
    group_width = group * HD
    half = token_rows
    length = (resumed[r] + (S - 1 - s)) * PAGE

    loads = [
        pltpu.make_async_copy(resident_keys, kv.at[pl.ds(0, held), :, pl.ds(0, kw)], load_sem.at[0]),
        pltpu.make_async_copy(resident_vals, kv.at[pl.ds(0, held), :, pl.ds(kw, kw)], load_sem.at[1]),
        pltpu.make_async_copy(w_query, wcat.at[:, pl.ds(0, qw)], load_sem.at[2]),
        pltpu.make_async_copy(w_keyval, wcat.at[:, pl.ds(qw, 2 * kw)], load_sem.at[3]),
        pltpu.make_async_copy(w_out, wout, load_sem.at[4]),
    ]
    for load in loads:
        load.start()

    barrier = pltpu.get_barrier_semaphore()

    def greet(o, carry):
        d = lax.rem(me + o, dests)
        pl.semaphore_signal(
            barrier, inc=1, device_id={"rollout": d // S, "section": lax.rem(d, S)}, device_id_type=MESH
        )
        return carry

    lax.fori_loop(1, dests, greet, 0)
    pl.semaphore_signal(barrier, inc=1, device_id={"tensor": other}, device_id_type=MESH)

    own_x[0] = entering[...]

    @pl.when(s == 0)
    def _():
        for k in range(1, BLOCKS):
            own_x[k] = arriving[k - 1]

    spare = kv.shape[0] - held
    kv[pl.ds(held, spare)] = jnp.zeros((spare, PAGE, 2 * kw), jnp.bfloat16)
    pl.semaphore_wait(barrier, dests)

    def cols(c, size=CHUNK):
        return pl.ds(pl.multiple_of(c * size, size), size)

    def rows_of(b):
        return pl.ds(pl.multiple_of(b * BLOCK, BLOCK), BLOCK)

    def fwd(k, c):
        return remote(own_x.at[k, :, cols(c)], peer_x.at[:, cols(c)], fwd_s.at[c], fwd_r.at[c], tensor=other)

    def hand(k, c):
        return remote(
            out.at[k, :, cols(c)],
            own_x.at[k + 1, :, cols(c)],
            hand_s.at[k, c],
            hand_r.at[k, c],
            section=jnp.minimum(s + 1, S - 1),
        )

    def ahead(j):
        return lax.rem(r + j, R)

    def behind(j):
        return lax.rem(r + R - j, R)

    def sq(j):
        return remote(
            squares.at[rows_of(ahead(j))], squares_in.at[rows_of(r)], sq_s.at[j], sq_r.at[j], rollout=ahead(j)
        )

    def rs(c, j):
        return remote(
            part.at[rows_of(ahead(j)), cols(c)],
            part_in.at[rows_of(r), cols(c)],
            rs_s.at[c, j],
            rs_r.at[c, j],
            rollout=ahead(j),
        )

    def ag(c, j):
        ref = attended.at[rows_of(r), cols(c, group_width)]
        return remote(ref, ref, ag_s.at[c, j], ag_r.at[c, j], rollout=ahead(j))

    def ex(c):
        return remote(
            mixed.at[pl.ds(pl.multiple_of(other * half, BLOCK), half), cols(c)],
            mixed_in.at[:, cols(c)],
            ex_s.at[c],
            ex_r.at[c],
            tensor=other,
        )

    def ship(o):
        to_r = lax.rem(r + o // S, R)
        to_s = lax.rem(s + lax.rem(o, S), S)
        return remote(
            packed.at[to_r * S + to_s], landed.at[me], ship_s.at[o], ship_r.at[o], rollout=to_r, section=to_s
        )

    def ship_mixed(low, high):
        def one(m, carry):
            ship((m // (S - 1) + 1) * S + lax.rem(m, S - 1) + 1).start()
            return carry

        lax.fori_loop(low, high, one, 0)

    def fz(k, j):
        return remote(
            kv.at[held + k], fresh.at[k, r, s], fz_s.at[k, j], fz_r.at[k, j], section=lax.rem(s + j, S)
        )

    def fx(k, j):
        return remote(fresh.at[k, r], fresh.at[k, r], fx_s.at[k, j], fx_r.at[k, j], rollout=ahead(j))

    def own_page(k):
        return pltpu.make_async_copy(kv.at[held + k], fresh.at[k, r, s], own_sem.at[k])

    own_slots = pltpu.make_async_copy(packed.at[me], landed.at[me], own_sem.at[BLOCKS])

    def spread(k):
        own_page(k).wait()
        for j in range(1, S):
            fz(k, j).wait()
        for j in range(1, R):
            fx(k, j).start()

    mixed_count = (R - 1) * (S - 1)
    loads[0].wait()
    loads[1].wait()

    def pack(d, carry):
        for c in range(packed.shape[1]):
            packed[d, c] = kv[pack_pages[d * packed.shape[1] + c]]
        return carry

    lax.fori_loop(0, dests, pack, 0)
    own_slots.start()
    for o in range(1, S):
        ship(jnp.int32(o)).start()

    def ship_plane(o, carry):
        ship(o * S).start()
        return carry

    lax.fori_loop(1, R, ship_plane, 0)

    def step_body(k, carry):
        for c in range(n_out):
            @pl.when((k > 0) & (s > 0))
            def _(c=c):
                hand(k - 1, c).wait_recv()

            fwd(k, c).start()

        def norm(ref, base):
            def body(i, carry):
                xf = ref[rows_of(i), :].astype(jnp.float32)
                ms = jnp.sum(xf * xf, axis=1, keepdims=True) / width
                rows = pl.ds(pl.multiple_of(base + i * BLOCK, BLOCK), BLOCK)
                normed[rows, :] = (xf * lax.rsqrt(ms + EPS) * gain[...].astype(jnp.float32)).astype(
                    jnp.bfloat16
                )
                squares[rows, :] = jnp.broadcast_to(ms, (BLOCK, HD))
                return carry

            lax.fori_loop(0, half // BLOCK, body, 0)

        norm(own_x.at[k], t * half)
        for c in range(n_out):
            fwd(k, c).wait()
        norm(peer_x, other * half)
        for j in range(1, R):
            sq(j).start()

        @pl.when(k == 0)
        def _():
            for load in loads[2:4]:
                load.wait()

        def project(c, carry):
            part[:, cols(c)] = jnp.dot(
                normed[...], wcat[:, cols(c)], preferred_element_type=jnp.float32
            ).astype(jnp.bfloat16)
            for j in range(1, R):
                rs(c, j).start()
            return carry

        lax.fori_loop(0, n_rs, project, 0)

        @pl.when(k == 1)
        def _():
            ship_mixed(mixed_count * 2 // 9, mixed_count * 4 // 9)

        for j in range(1, R):
            sq(j).wait()
        ms = [squares[rows_of(r), :]] + [squares_in[rows_of(behind(j)), :] for j in range(1, R)]
        whole = lax.rsqrt(sum(ms) / R + EPS)
        ratios = []
        for m in ms:
            local = lax.rsqrt(m + EPS)
            ratios.append(jnp.where(local > 0, whole / jnp.where(local > 0, local, 1.0), 0.0)[:, :1])
        angle = (length + k * BLOCK + lax.broadcasted_iota(jnp.int32, (BLOCK, HD), 0)).astype(
            jnp.float32
        ) * freq[...]
        lane = lax.broadcasted_iota(jnp.int32, (BLOCK, HD), 1)
        cos = jnp.cos(angle)
        sin = jnp.sin(angle)
        sin = jnp.where(lane < HD // 2, -sin, sin)

        def rotate(v):
            return v * cos + pltpu.roll(v, HD // 2, 1) * sin

        shifts = keyval_bias[...].astype(jnp.float32)
        for c in range(n_rs):
            for j in range(1, R):
                rs(c, j).wait()
            acc = part[rows_of(r), cols(c)].astype(jnp.float32) * ratios[0]
            for j in range(1, R):
                acc = acc + part_in[rows_of(behind(j)), cols(c)].astype(jnp.float32) * ratios[j]
            low = c * CHUNK
            for h in range(CHUNK // HD):
                at = low + h * HD
                one = acc[:, h * HD : (h + 1) * HD]
                if at < qw:
                    one = rotate(one + query_bias[:, at : at + HD].astype(jnp.float32))
                    heads[at // HD * BLOCK : (at // HD + 1) * BLOCK, :] = one.astype(jnp.bfloat16)
                else:
                    at = at - qw
                    one = one + shifts[at // kw : at // kw + 1, at % kw : at % kw + HD]
                    if at < kw:
                        one = rotate(one)
                    kv[held + k, :, at : at + HD] = one.astype(jnp.bfloat16)
        own_page(k).start()
        for j in range(1, S):
            fz(k, j).start()

        @pl.when(k == BLOCKS - 1)
        def _():
            ship_mixed(mixed_count * 7 // 9, mixed_count)

        total = kv.shape[0] * PAGE
        column = lax.broadcasted_iota(jnp.int32, (group * BLOCK, total), 1)
        token = lax.rem(lax.broadcasted_iota(jnp.int32, (group * BLOCK, total), 0), BLOCK)
        seen = (column < length) | ((column >= context) & (column - context <= k * BLOCK + token))
        scale = math.log2(math.e) / math.sqrt(HD)

        def score(g):
            return lax.dot_general(
                heads[g * group * BLOCK : (g + 1) * group * BLOCK, :],
                kv[:, :, g * HD : (g + 1) * HD].reshape(total, HD),
                (((1,), (1,)), ((), ())),
                preferred_element_type=jnp.float32,
            )

        upcoming = score(0)
        for g in range(n_kv):
            at = g * HD
            scores = jnp.where(seen, upcoming, -1e30)
            if g + 1 < n_kv:
                upcoming = score(g + 1)
            powers = jnp.exp2((scores - jnp.max(scores, axis=-1, keepdims=True)) * scale)
            total_power = jnp.sum(powers, axis=-1, keepdims=True)
            got = jnp.dot(
                powers.astype(jnp.bfloat16),
                kv[:, :, kw + at : kw + at + HD].reshape(total, HD),
                preferred_element_type=jnp.float32,
            )
            got = (got / total_power).astype(jnp.bfloat16)
            for i in range(group):
                lane = (g * group + i) * HD
                attended[rows_of(r), lane : lane + HD] = got[i * BLOCK : (i + 1) * BLOCK, :]
            for j in range(1, R):
                ag(g, j).start()

        @pl.when(k == 0)
        def _():
            loads[4].wait()

        @pl.when(k == BLOCKS - 1)
        def _():
            spread(BLOCKS - 1)

        for g in range(n_kv):
            for j in range(1, R):
                ag(g, j).wait()

        active = layer_on[s].astype(jnp.float32)

        def finish(c):
            ex(c).wait()
            own = mixed[pl.ds(pl.multiple_of(t * half, BLOCK), half), cols(c)].astype(jnp.float32)
            summed = own + mixed_in[:, cols(c)].astype(jnp.float32)
            base = own_x[k, :, cols(c)].astype(jnp.float32)
            out[k, :, cols(c)] = (base + active * summed).astype(jnp.bfloat16)

            @pl.when((k < BLOCKS - 1) & (s < S - 1))
            def _():
                hand(k, c).start()

        def project_out(c, carry):
            mixed[:, cols(c)] = jnp.dot(
                attended[...], wout[:, cols(c)], preferred_element_type=jnp.float32
            ).astype(jnp.bfloat16)
            ex(c).start()

            @pl.when(c > 0)
            def _():
                finish(c - 1)

            return carry

        lax.fori_loop(0, n_out, project_out, 0)
        finish(jnp.int32(n_out - 1))

        @pl.when(k < BLOCKS - 1)
        def _():
            spread(k)

        @pl.when(k == 0)
        def _():
            ship_mixed(0, mixed_count * 2 // 9)

        @pl.when(k == 1)
        def _():
            ship_mixed(mixed_count * 4 // 9, mixed_count * 7 // 9)

        return carry

    lax.fori_loop(0, BLOCKS, step_body, 0)

    @pl.when(s < S - 1)
    def _():
        for k in range(BLOCKS - 1):
            for c in range(n_out):
                hand(k, c).wait_send()

    def ship_wait(o, carry):
        ship(o).wait()
        return carry

    lax.fori_loop(1, dests, ship_wait, 0)
    own_slots.wait()
    for k in range(BLOCKS):
        for j in range(1, R):
            fx(k, j).wait()


def place_kernel(slots, kind, place, landed, fresh, pool):
    def body(i, carry):
        @pl.when(kind[i] == 0)
        def _():
            pool[i] = jnp.zeros_like(pool[i])

        @pl.when(kind[i] == 1)
        def _():
            pool[i] = landed[place[i]]

        @pl.when(kind[i] == 2)
        def _():
            pool[i] = fresh[place[i]]

        return carry

    lax.fori_loop(0, slots, body, 0)


def local(
    entering,
    arriving,
    w_query,
    w_keyval,
    w_out,
    query_bias,
    keyval_bias,
    norm_gain,
    resident_kv,
    resumed_pages,
    section_active,
    block_table,
):
    R = lax.axis_size("rollout")
    S = lax.axis_size("section")
    r = lax.axis_index("rollout")
    s = lax.axis_index("section")
    width_block, qw = w_query.shape[1:]
    kw = w_keyval.shape[3]
    token_rows = entering.shape[1]
    rows = R * BLOCK
    out_width = w_out.shape[2]
    context = resident_kv.shape[2]
    page_count = block_table.shape[2]
    dests = R * S
    cap = (page_count + dests - 1) // dests
    me = r * S + s

    routing = block_table.reshape(dests, page_count, 2)
    targets = routing[:, :, 0]
    slot_ids = routing[:, :, 1]
    page_ids = jnp.arange(page_count, dtype=jnp.int32)
    before = page_ids[None, :] < page_ids[:, None]
    ranks = jnp.sum(
        ((targets[:, :, None] == targets[:, None, :]) & before[None]).astype(jnp.int32), axis=2
    )
    column = targets[me] * cap + ranks[me]
    buffer_ids = jnp.arange(dests * cap, dtype=jnp.int32)
    source_pages = jnp.minimum(page_ids, context // PAGE - 1)
    pack_pages = jnp.sum(
        jnp.where(buffer_ids[:, None] == column[None, :], source_pages[None, :], 0), axis=1
    ).astype(jnp.int32)
    sources = jnp.arange(dests, dtype=jnp.int32)
    first_of = (resumed_pages[:, None] + (S - 1 - jnp.arange(S, dtype=jnp.int32))[None, :]).reshape(-1)
    switched_on = jnp.broadcast_to(section_active[None, :], (R, S)).reshape(-1) > 0
    turn = page_ids[None, :] - first_of[:, None]
    alive = (turn < BLOCKS) & switched_on[:, None]
    kinds = jnp.where(alive, jnp.where(turn >= 0, 2, 1), 0)
    places = jnp.where(
        kinds == 2,
        jnp.clip(turn, 0, BLOCKS - 1) * dests + sources[:, None],
        sources[:, None] * cap + jnp.minimum(ranks, cap - 1),
    )
    codes = (kinds * (BLOCKS * dests + dests * cap) + places).reshape(-1)
    hit = (targets == me).reshape(-1)[None, :] & (slot_ids.reshape(-1)[None, :] == page_ids[:, None])
    code = jnp.sum(jnp.where(hit, codes[None, :], 0), axis=1).astype(jnp.int32)
    base = BLOCKS * dests + dests * cap
    kind, place = code // base, code % base

    freq = np.power(1000000.0, -np.arange(HD // 2) * (2.0 / HD)).astype(np.float32)
    freq = jnp.asarray(np.concatenate([freq, freq])[None, :])

    resident = resident_kv[0, 0].reshape(context // PAGE, PAGE, 2, kw)
    page_shape = (PAGE, 2 * kw)
    bf16 = jnp.bfloat16
    f32 = jnp.float32
    anywhere = pl.BlockSpec(memory_space=pl.ANY)
    vmem = pl.BlockSpec(memory_space=pltpu.VMEM)
    smem = pl.BlockSpec(memory_space=pltpu.SMEM)
    dma = pltpu.SemaphoreType.DMA

    total = -(-(context + BLOCKS * BLOCK) // HD) * HD
    n_rs = (qw + 2 * kw) // CHUNK
    n_out = out_width // CHUNK
    n_kv = kw // HD
    section_out, landed, fresh = pl.pallas_call(
        functools.partial(steps_kernel, (R, S, context)),
        out_shape=(
            jax.ShapeDtypeStruct((BLOCKS, token_rows, out_width), bf16),
            jax.ShapeDtypeStruct((dests, cap) + page_shape, bf16),
            jax.ShapeDtypeStruct((BLOCKS, R, S) + page_shape, bf16),
        ),
        in_specs=[smem] * 3 + [vmem] * 6 + [anywhere] * 5,
        out_specs=(vmem, anywhere, vmem if dests <= 16 else anywhere),
        scratch_shapes=[
            pltpu.VMEM((width_block, qw + 2 * kw), bf16),
            pltpu.VMEM((qw, out_width), bf16),
            pltpu.VMEM((total // PAGE,) + page_shape, bf16),
            pltpu.VMEM((dests, cap) + page_shape, bf16),
            pltpu.VMEM((BLOCKS, token_rows, width_block), bf16),
            pltpu.VMEM((token_rows, width_block), bf16),
            pltpu.VMEM((rows, width_block), bf16),
            pltpu.VMEM((rows, qw + 2 * kw), bf16),
            pltpu.VMEM((rows, HD), f32),
            pltpu.VMEM((rows, qw + 2 * kw), bf16),
            pltpu.VMEM((rows, HD), f32),
            pltpu.VMEM((qw // HD * BLOCK, HD), bf16),
            pltpu.VMEM((rows, qw), bf16),
            pltpu.VMEM((rows, out_width), bf16),
            pltpu.VMEM((token_rows, out_width), bf16),
            dma((5,)),
            dma((n_out,)),
            dma((n_out,)),
            dma((R,)),
            dma((R,)),
            dma((n_rs, R)),
            dma((n_rs, R)),
            dma((n_kv, R)),
            dma((n_kv, R)),
            dma((n_out,)),
            dma((n_out,)),
            dma((BLOCKS, n_out)),
            dma((BLOCKS, n_out)),
            dma((dests,)),
            dma((dests,)),
            dma((BLOCKS, S)),
            dma((BLOCKS, S)),
            dma((BLOCKS, R)),
            dma((BLOCKS, R)),
            dma((BLOCKS + 1,)),
        ],
        compiler_params=pltpu.CompilerParams(
            collective_id=0, has_side_effects=True, vmem_limit_bytes=60 * 1024 * 1024
        ),
        name="relay_steps",
    )(
        resumed_pages,
        section_active,
        pack_pages,
        entering[0],
        arriving,
        norm_gain,
        query_bias,
        keyval_bias[0],
        freq,
        w_query[0],
        w_keyval[0].reshape(width_block, 2 * kw),
        w_out[0],
        resident[:, :, 0],
        resident[:, :, 1],
    )

    pool = pl.pallas_call(
        functools.partial(place_kernel, page_count),
        out_shape=jax.ShapeDtypeStruct((page_count,) + page_shape, bf16),
        in_specs=[smem, smem, vmem, vmem],
        out_specs=vmem,
        compiler_params=pltpu.CompilerParams(vmem_limit_bytes=48 * 1024 * 1024),
        name="place_pages",
    )(
        kind,
        place,
        landed.reshape((dests * cap,) + page_shape),
        fresh.reshape((BLOCKS * dests,) + page_shape),
    )
    return (section_out[None], pool.reshape(1, 1, page_count, PAGE, 2, kw))


def solution(mesh):
    in_specs = (
        P("section", "tensor", "rollout"),
        P(None, "tensor", "rollout"),
        P("section", "rollout", "tensor"),
        P("section", "rollout", None, "tensor"),
        P("section", "tensor", "rollout"),
        P("section", "tensor"),
        P("section", None, "tensor"),
        P("section", "rollout"),
        P("rollout", "section", None, None, "tensor"),
        P(),
        P(),
        P(),
    )
    out_specs = (
        P("section", None, "tensor", "rollout"),
        P("rollout", "section", None, None, None, "tensor"),
    )
    return jax.shard_map(local, mesh=mesh, in_specs=in_specs, out_specs=out_specs, check_vma=False)
```
